256 devices in a mesh: seq: 64 (over z, x, core), dp: 4 (over y).
Axes of the slice: x: 4, y: 4, z: 8, core: 2. Of those that a mesh axis runs over, the one named last changes fastest.
Arguments:
- qkv: bfloat16 [4, 16384, 3, 512], P('dp', 'seq'), may hold values from -16 to 16
- dout: bfloat16 [4, 16384, 1024], P('dp', 'seq'), may hold values from -6 to 6
- out_weight: bfloat16 [512, 1024], replicated, may hold values from -0.25 to 0.25
- head_offsets: int32 [2, 8], replicated, may hold values from 0 to 15, as said below
Outputs:
- grad_qkv: bfloat16 [4, 16384, 3, 512], P('dp', 'seq')
- weight_grad: float32 [512, 1024], P('seq')
The draws below stay inside these ranges and needn't reach their ends.
Inputs may be any that keep to these rules, and one draw needn't show every extreme that they name: `head_offsets`: row 0 holds values below 4, row 1 values below 16; each row holds 0 and its largest allowed value.
All inputs are finite; a program needn't handle non-finite values.
Results may differ from the reference program's by a relative error of at most 0.02.
Values may be sent and summed in bfloat16 or wider, within the bound.
A program may use at most 64 MiB of HBM per device.

```python
import functools
import jax
import jax.numpy as jnp
from jax import lax

D = 1024
H = 8
E = 64
W1 = 256
R2 = 4
R3 = 16
W2 = 1024
W3 = 4096
SEQ_LEN = 16384
SLIDES = 4


def draw_qkv(key, part):
    key = jax.random.fold_in(key, 3)
    base_key = jax.random.fold_in(key, 0)
    full_shape = (SLIDES, SEQ_LEN, 3, H * E)
    column_scale = jnp.array([1.3, 1.3, 1.0], jnp.float32)[None, None, :, None]
    drawn_values = jax.random.truncated_normal(base_key, -4.5, 4.5, full_shape, jnp.float32) * column_scale
    return drawn_values.astype(jnp.bfloat16)


def draw_head_offsets(key, part):
    key = jax.random.fold_in(key, 7)
    near_key, far_key, order_near, order_far = jax.random.split(key, 4)
    near_row = jax.random.randint(near_key, (H,), 0, R2)
    far_row = jax.random.randint(far_key, (H,), 0, R3)
    near_order = jax.random.permutation(order_near, H)
    far_order = jax.random.permutation(order_far, H)
    near_row = near_row.at[near_order[0]].set(R2 - 1).at[near_order[1]].set(0)
    far_row = far_row.at[far_order[0]].set(R3 - 1).at[far_order[1]].set(0)
    return jnp.stack([near_row, far_row]).astype(jnp.int32)


def shard_levels(stream_key, dims, cuts, low, largest):
    factor_of = 1.0
    for dim, blocks in cuts:
        draws = jax.random.uniform(jax.random.fold_in(jax.random.fold_in(stream_key, 6), dim), (blocks,), jnp.float32, low / len(cuts), largest / len(cuts))
        factor_of = factor_of * jnp.repeat(jnp.exp(draws), dims[dim] // blocks).reshape((-1,) + (1,) * (len(dims) - 1 - dim))
    return factor_of


def scatter_about(own_key, dims, width, reach, pieces=(), held_as=jnp.bfloat16):
    drawn = width * jax.random.normal(own_key, dims, jnp.float32)
    if pieces:
        drawn = drawn * shard_levels(own_key, dims, pieces, -0.22, 0.18)
    return jnp.clip(drawn, -reach, reach).astype(held_as)


def setup_inputs(seed: int = 0) -> dict:
    splits = jax.random.split(jax.random.key(seed), 5)
    return {
        "qkv": draw_qkv(jax.random.fold_in(splits[4], 71), 0),
        "dout": scatter_about(splits[1], (SLIDES, SEQ_LEN, D), 1.0, 6.0, ((0, 4), (1, 64))),
        "out_weight": scatter_about(splits[2], (H * E, D), (H * E) ** -0.5, 0.25),
        "head_offsets": draw_head_offsets(jax.random.fold_in(splits[4], 71), 0),
    }


def residue_mask(dilation, offsets_row):
    return jnp.arange(dilation)[:, None] == offsets_row[None, :]


def pick_every(array, dilation, offsets_row):
    shaped = array.reshape((array.shape[0] // dilation, dilation) + array.shape[1:])
    mask = residue_mask(dilation, offsets_row).reshape((1, dilation, H) + (1,) * (array.ndim - 2))
    return jnp.sum(jnp.where(mask, shaped, jnp.zeros_like(shaped)), axis=1)


def spread_every(array, dilation, offsets_row, filler):
    mask = residue_mask(dilation, offsets_row).reshape((1, dilation, H) + (1,) * (array.ndim - 2))
    widened = jnp.where(mask, array[:, None], jnp.asarray(filler, array.dtype))
    return widened.reshape((array.shape[0] * dilation,) + array.shape[1:])


def block_forward(query_rows, key_rows, value_rows):
    score_scale = E ** -0.5
    scores = jnp.einsum("qhe,khe->hqk", query_rows.astype(jnp.float32), key_rows.astype(jnp.float32)) * score_scale
    row_max = jnp.max(scores, axis=2)
    weights = jnp.exp(scores - row_max[:, :, None])
    row_total = jnp.sum(weights, axis=2)
    rounded = lax.optimization_barrier(weights.astype(jnp.bfloat16)).astype(jnp.float32)
    weighted = jnp.einsum("hqk,khe->qhe", rounded, value_rows.astype(jnp.float32))
    return row_max.T, row_total.T, weighted


def block_backward(query_rows, key_rows, value_rows, grad_rows, log_totals, grad_dots):
    score_scale = E ** -0.5
    scores = jnp.einsum("qhe,khe->hqk", query_rows.astype(jnp.float32), key_rows.astype(jnp.float32)) * score_scale
    probabilities = jnp.exp(scores - log_totals.T[:, :, None])
    grad_probs = jnp.einsum("qhe,khe->hqk", grad_rows.astype(jnp.float32), value_rows.astype(jnp.float32))
    grad_scores = probabilities * (grad_probs - grad_dots.T[:, :, None])
    probs_low = lax.optimization_barrier(probabilities.astype(jnp.bfloat16)).astype(jnp.float32)
    scores_low = lax.optimization_barrier(grad_scores.astype(jnp.bfloat16)).astype(jnp.float32)
    grad_values = jnp.einsum("hqk,qhe->khe", probs_low, grad_rows.astype(jnp.float32))
    grad_queries = jnp.einsum("hqk,khe->qhe", scores_low, key_rows.astype(jnp.float32)) * score_scale
    grad_keys = jnp.einsum("hqk,qhe->khe", scores_low, query_rows.astype(jnp.float32)) * score_scale
    return grad_queries, grad_keys, grad_values


def branch_forward(query_rows, key_rows, value_rows, span_rows):
    segment_count = query_rows.shape[0] // span_rows
    shaped = tuple(array.reshape(segment_count, span_rows, H, E) for array in (query_rows, key_rows, value_rows))
    row_max, row_total, weighted = lax.map(lambda block_items: block_forward(*block_items), shaped)
    return row_max.reshape(-1, H), row_total.reshape(-1, H), weighted.reshape(-1, H, E)


def branch_backward(query_rows, key_rows, value_rows, grad_rows, log_totals, grad_dots, span_rows):
    segment_count = query_rows.shape[0] // span_rows
    shaped = tuple(array.reshape(segment_count, span_rows, H, E) for array in (query_rows, key_rows, value_rows, grad_rows))
    stats = tuple(array.reshape(segment_count, span_rows, H) for array in (log_totals, grad_dots))
    grad_queries, grad_keys, grad_values = lax.map(lambda block_items: block_backward(*block_items), shaped + stats)
    return grad_queries.reshape(-1, H, E), grad_keys.reshape(-1, H, E), grad_values.reshape(-1, H, E)


def one_slide(qkv_slide, dout_slide, out_weight, head_offsets):
    length = qkv_slide.shape[0]
    query_rows = qkv_slide[:, 0].reshape(length, H, E)
    key_rows = qkv_slide[:, 1].reshape(length, H, E)
    value_rows = qkv_slide[:, 2].reshape(length, H, E)
    branch_plans = ((1, W1, None), (R2, W2 // R2, head_offsets[0]), (R3, W3 // R3, head_offsets[1]))
    maxima_list, totals_list, weighted_list = [], [], []
    for dilation, span_rows, offsets_row in branch_plans:
        if dilation == 1:
            picked = (query_rows, key_rows, value_rows)
        else:
            picked = tuple(pick_every(array, dilation, offsets_row) for array in (query_rows, key_rows, value_rows))
        row_max, row_total, weighted = branch_forward(picked[0], picked[1], picked[2], span_rows)
        if dilation > 1:
            row_max = spread_every(row_max, dilation, offsets_row, -jnp.inf)
            row_total = spread_every(row_total, dilation, offsets_row, 0.0)
            weighted = spread_every(weighted, dilation, offsets_row, 0.0)
        maxima_list.append(row_max)
        totals_list.append(row_total)
        weighted_list.append(weighted)
    row_peak = functools.reduce(jnp.maximum, maxima_list)
    factors = [jnp.exp(row_max - row_peak) for row_max in maxima_list]
    row_denom = factors[0] * totals_list[0] + factors[1] * totals_list[1] + factors[2] * totals_list[2]
    blended = factors[0][:, :, None] * weighted_list[0] + factors[1][:, :, None] * weighted_list[1] + factors[2][:, :, None] * weighted_list[2]
    combined = blended / row_denom[:, :, None]
    log_totals = row_peak + jnp.log(row_denom)
    attention = combined.reshape(length, H * E).astype(jnp.bfloat16)
    grad_attn = jnp.dot(dout_slide, out_weight.T, preferred_element_type=jnp.float32).astype(jnp.bfloat16)
    grad_dots = jnp.sum(grad_attn.astype(jnp.float32).reshape(length, H, E) * attention.astype(jnp.float32).reshape(length, H, E), axis=2)
    weight_part = jnp.dot(attention.T, dout_slide, preferred_element_type=jnp.float32)
    grad_heads = grad_attn.reshape(length, H, E)
    grad_query_sum = jnp.zeros((length, H, E), jnp.float32)
    grad_key_sum = jnp.zeros((length, H, E), jnp.float32)
    grad_value_sum = jnp.zeros((length, H, E), jnp.float32)
    for dilation, span_rows, offsets_row in branch_plans:
        if dilation == 1:
            picked = (query_rows, key_rows, value_rows, grad_heads, log_totals, grad_dots)
        else:
            picked = tuple(pick_every(array, dilation, offsets_row) for array in (query_rows, key_rows, value_rows, grad_heads, log_totals, grad_dots))
        branch_grads = branch_backward(picked[0], picked[1], picked[2], picked[3], picked[4], picked[5], span_rows)
        if dilation > 1:
            branch_grads = tuple(spread_every(array, dilation, offsets_row, 0.0) for array in branch_grads)
        grad_query_sum = grad_query_sum + branch_grads[0]
        grad_key_sum = grad_key_sum + branch_grads[1]
        grad_value_sum = grad_value_sum + branch_grads[2]
    stacked = jnp.stack([grad_query_sum, grad_key_sum, grad_value_sum], axis=1).reshape(length, 3, H * E)
    return stacked.astype(jnp.bfloat16), weight_part


def reference(qkv, dout, out_weight, head_offsets):
    grad_qkv, slide_parts = lax.map(lambda slide_items: one_slide(slide_items[0], slide_items[1], out_weight, head_offsets), (qkv, dout))
    return grad_qkv, jnp.sum(slide_parts, axis=0) / SLIDES
```

```python
import jax
import jax.numpy as jnp
from jax import lax
from jax.experimental import pallas as pl
from jax.experimental.pallas import tpu as pltpu
from jax.sharding import PartitionSpec as P

XS, ZS, YS = 4, 8, 4
T = 256
E = 64
C2 = 0.125 * 1.4426950408889634
F32, BF16 = jnp.float32, jnp.bfloat16
NEG = -3.0e38


def dot(a, b):
    return lax.dot_general(a, b, (((1,), (0,)), ((), ())), preferred_element_type=F32)


def dot_nt(a, b):
    return lax.dot_general(a, b, (((1,), (1,)), ((), ())), preferred_element_type=F32)


def dot_tn(a, b):
    return lax.dot_general(a, b, (((0,), (0,)), ((), ())), preferred_element_type=F32)


def kernel(
    qkv_ref, dout_ref, w_ref, off_ref, out_ref, wg_ref,
    qkv_in, dout2, wv, perm, x, oth, sibs, sibr, kn, ns, kf, fs, qn, qf, g,
    o1, t1, m1, o2, t2, m2, o3, t3, m3, p1, pn, pf, attn,
    g1, d1, g2, d2, g3, d3, acc, nsend, nrecv, fsend, frecv,
    wgs, wgr, zsb, zr, ysb, yr,
    load_sem, sib_s, sib_r, near_s, near_r, far_s, far_r, x_s, x_r, z_s, z_r, y_s, y_r,
):
    pos = lax.axis_index("seq")
    y = lax.axis_index("dp")
    c = pos % 2
    xx = (pos // 2) % XS
    z = pos // (2 * XS)
    chip = (z % 2) * XS + xx

    def at(z_, x_, c_):
        return (z_ * XS + x_) * 2 + c_

    def far_pos(d, r):
        ch = (chip + d + 8) % 8
        return at(z - z % 2 + ch // XS, ch % XS, (c + r) % 2)

    xp = xx + 1 - 2 * (xx % 2)
    sib = at(z, xx, 1 - c)

    def near_pos(r):
        return at(z, xp, (c + r) % 2)

    y_target = at(4 * c + z // 2, xx, (z + 1) % 2)
    y_source = at(2 * (z % 4) + (c + 1) % 2, xx, z // 4)

    def remote(src, dst, send, recv, target, row=None):
        where = {"seq": target} if row is None else {"seq": target, "dp": row}
        return pltpu.make_async_remote_copy(
            src_ref=src, dst_ref=dst, send_sem=send, recv_sem=recv,
            device_id=where, device_id_type=pl.DeviceIdType.MESH,
        )

    mine = pl.multiple_of(c * 256, 256)
    theirs = pl.multiple_of((1 - c) * 256, 256)
    load_qkv = pltpu.make_async_copy(qkv_ref, qkv_in, load_sem.at[0])
    load_dout = pltpu.make_async_copy(dout_ref, dout2.at[0], load_sem.at[1])
    load_w = pltpu.make_async_copy(w_ref.at[pl.ds(mine, 256), :], wv, load_sem.at[2])
    load_qkv.start()
    load_dout.start()
    load_w.start()

    barrier = pltpu.get_barrier_semaphore()

    def greet(target, row=None):
        where = {"seq": target} if row is None else {"seq": target, "dp": row}
        pl.semaphore_signal(
            barrier, inc=1, device_id=where, device_id_type=pl.DeviceIdType.MESH
        )

    greet(sib)
    for d in range(1, 8):
        for r in range(2):
            greet(far_pos(d, r))
    for d in range(1, ZS):
        greet(at((z + d) % ZS, xx, c))
    for d in range(YS):
        greet(y_source, (y + d) % YS)

    lane = lax.broadcasted_iota(jnp.int32, (1, 128), 1)
    low_lane = lane < E
    head_mask = [low_lane.astype(F32).astype(BF16), (lane >= E).astype(F32).astype(BF16)]

    def offsets(row, half, pair):
        first = 4 * half + 2 * pair
        return jnp.where(low_lane, off_ref[row, first], off_ref[row, first + 1])

    def near_rows(array, off):
        shaped = array.reshape(4, 4, 16, 128)
        parts = [shaped[:, k] * (off == k).astype(F32).astype(array.dtype) for k in range(4)]
        return ((parts[0] + parts[1]) + (parts[2] + parts[3])).reshape(64, 128)

    def far_rows(array, off):
        shaped = array.reshape(16, 16, 128)
        total = shaped[0] * (off == 0).astype(F32).astype(array.dtype)
        for k in range(1, 16):
            total = total + shaped[k] * (off == k).astype(F32).astype(array.dtype)
        return total

    def near_spread(array, off):
        shaped = array.reshape(4, 1, 16, 128)
        parts = [jnp.where((off == k).reshape(1, 1, 1, 128), shaped, 0.0) for k in range(4)]
        return jnp.concatenate(parts, axis=1).reshape(T, 128)

    def far_spread(array, off):
        parts = [jnp.where(off == k, array, 0.0) for k in range(16)]
        return jnp.concatenate(parts, axis=0)

    row_id = lax.broadcasted_iota(jnp.int32, (T, T), 0)
    col_id = lax.broadcasted_iota(jnp.int32, (T, T), 1)
    swapped = (row_id % 16) * 16 + row_id // 16
    perm[...] = (swapped == col_id).astype(F32).astype(BF16)

    load_qkv.wait()
    for t in range(3):
        own = dot(perm[...], qkv_in[t, :, pl.ds(mine, 256)]).astype(BF16)
        x[0, t, 0] = own[:, :128]
        x[0, t, 1] = own[:, 128:]
        other = dot(perm[...], qkv_in[t, :, pl.ds(theirs, 256)]).astype(BF16)
        oth[t, 0] = other[:, :128]
        oth[t, 1] = other[:, 128:]
    for p in range(2):
        near_own, far_own = offsets(0, c, p), offsets(1, c, p)
        near_other, far_other = offsets(0, 1 - c, p), offsets(1, 1 - c, p)
        for k in range(2):
            kn[0, k, p] = near_rows(x[0, 1 + k, p], near_own)
            kf[0, k, p] = far_rows(x[0, 1 + k, p], far_own)
            ns[k, p] = near_rows(oth[1 + k, p], near_other)
            fs[k, p] = far_rows(oth[1 + k, p], far_other)
        qn[p, 0] = near_rows(x[0, 0, p], near_own)
        qf[p, 0] = far_rows(x[0, 0, p], far_own)
    pl.semaphore_wait(barrier, 15 + (ZS - 1) + YS)

    sib_copy = remote(oth, x.at[1], sib_s.at[0], sib_r.at[0], sib)
    sib_copy.start()
    near_copies = []
    for r in range(2):
        copy = remote(
            kn.at[0] if r == 0 else ns, kn.at[2 + r], near_s.at[0, r], near_r.at[0, r], near_pos(r)
        )
        copy.start()
        near_copies.append(copy)
    far_copies = []
    for d in range(1, 8):
        for r in range(2):
            slot = 2 * (d - 1) + r
            copy = remote(
                kf.at[0] if r == 0 else fs, kf.at[2 + slot],
                far_s.at[0, slot], far_r.at[0, slot], far_pos(d, r),
            )
            copy.start()
            far_copies.append(copy)
    load_dout.wait()
    dout_copy = remote(dout2.at[0], dout2.at[1], sib_s.at[1], sib_r.at[1], sib)
    dout_copy.start()

    def forward(query, key, value, probs_ref):
        probs, maxima = [], []
        for h in range(2):
            scores = dot_nt(query, key * head_mask[h])
            row_max = jnp.max(scores, axis=1, keepdims=True)
            prob = jnp.exp2((scores - row_max) * C2).astype(BF16)
            probs_ref[h] = prob
            probs.append(prob)
            maxima.append(row_max * C2)
        ones = jnp.ones((T, 128), BF16)
        right = jnp.concatenate(
            [
                jnp.concatenate([value * head_mask[h], ones * head_mask[h]], axis=1)
                for h in range(2)
            ],
            axis=0,
        )
        both = dot(jnp.concatenate(probs, axis=1), right)
        return both[:, :128], both[:, 128:], jnp.where(low_lane, maxima[0], maxima[1])

    def dense_forward(s):
        def body(p, carry):
            out, total, peak = forward(x[s, 0, p], x[s, 1, p], x[s, 2, p], p1.at[s, p])
            o1[s, p], t1[s, p], m1[s, p] = out, total, peak
            return carry

        lax.fori_loop(0, 2, body, 0)

    def grad_in(s):
        grads = dot_nt(dout2[s], wv[...]).astype(BF16)
        moved = dot(perm[...], grads).astype(BF16)
        g[s, 0] = moved[:, :128]
        g[s, 1] = moved[:, 128:]

    dense_forward(0)
    load_w.wait()
    grad_in(0)
    sib_copy.wait()
    for p in range(2):
        near_own, far_own = offsets(0, c, p), offsets(1, c, p)
        for k in range(2):
            kn[1, k, p] = near_rows(x[1, 1 + k, p], near_own)
            kf[1, k, p] = far_rows(x[1, 1 + k, p], far_own)
        qn[p, 1] = near_rows(x[1, 0, p], near_own)
        qf[p, 1] = far_rows(x[1, 0, p], far_own)
    dense_forward(1)
    dout_copy.wait()
    grad_in(1)

    for copy in near_copies:
        copy.wait()

    def near_forward(p, carry):
        out, total, peak = forward(
            qn[p].reshape(128, 128), kn[:, 0, p].reshape(T, 128), kn[:, 1, p].reshape(T, 128),
            pn.at[p],
        )
        o2[p], t2[p], m2[p] = (a.reshape(2, 64, 128) for a in (out, total, peak))
        return carry

    lax.fori_loop(0, 2, near_forward, 0)
    for copy in far_copies:
        copy.wait()

    def far_forward(p, carry):
        out, total, peak = forward(
            qf[p].reshape(32, 128), kf[:, 0, p].reshape(T, 128), kf[:, 1, p].reshape(T, 128),
            pf.at[p],
        )
        o3[p], t3[p], m3[p] = (a.reshape(2, 16, 128) for a in (out, total, peak))
        return carry

    lax.fori_loop(0, 2, far_forward, 0)

    same_head = (
        (lax.broadcasted_iota(jnp.int32, (256, 128), 0) % 128 < E)
        == (lax.broadcasted_iota(jnp.int32, (256, 128), 1) < E)
    ).astype(F32).astype(BF16)

    def combine(p, s):
        near_off, far_off = offsets(0, c, p), offsets(1, c, p)

        def near_wide(array):
            return jnp.broadcast_to(array.reshape(4, 1, 16, 128), (4, 4, 16, 128)).reshape(T, 128)

        def far_wide(array):
            return jnp.broadcast_to(array.reshape(1, 16, 128), (16, 16, 128)).reshape(T, 128)

        parts = [
            jnp.where((near_off == k).reshape(1, 1, 1, 128), m2[p, s].reshape(4, 1, 16, 128), NEG)
            for k in range(4)
        ]
        max2 = jnp.concatenate(parts, axis=1).reshape(T, 128)
        max3 = jnp.concatenate([jnp.where(far_off == k, m3[p, s], NEG) for k in range(16)], axis=0)
        max1 = m1[s, p]
        peak = jnp.maximum(jnp.maximum(max1, max2), max3)
        e1, e2, e3 = jnp.exp2(max1 - peak), jnp.exp2(max2 - peak), jnp.exp2(max3 - peak)
        denom = e1 * t1[s, p] + e2 * near_wide(t2[p, s]) + e3 * far_wide(t3[p, s])
        inverse = 1.0 / denom
        f1, f2, f3 = e1 * inverse, e2 * inverse, e3 * inverse
        mixed = f1 * o1[s, p] + f2 * near_wide(o2[p, s]) + f3 * far_wide(o3[p, s])
        low = mixed.astype(BF16)
        grads = g[s, p].astype(F32)
        product = grads * low.astype(F32)
        high = product.astype(BF16)
        rest = (product - high.astype(F32)).astype(BF16)
        dstat = dot(jnp.concatenate([high, rest], axis=1), same_head)
        g1[s, p] = (grads * f1).astype(BF16)
        d1[s, p] = dstat * f1
        g2[p, s] = near_rows(grads * f2, near_off).astype(BF16)
        d2[p, s] = near_rows(dstat * f2, near_off)
        g3[p, s] = far_rows(grads * f3, far_off).astype(BF16)
        d3[p, s] = far_rows(dstat * f3, far_off)
        return low

    for s in range(2):
        rows = jnp.concatenate([combine(p, s) for p in range(2)], axis=1)
        attn[s * T : (s + 1) * T, :] = dot(perm[...], rows).astype(BF16)

    for k in range(4):
        columns = slice(256 * k, 256 * k + 256)
        both = dot_tn(attn[0:T, :], dout2[0, :, columns])
        both = both + dot_tn(attn[T:, :], dout2[1, :, columns])
        shaped = both.astype(BF16).reshape(4, 4, 16, 256)
        for to in range(XS):
            wgs[to, :, :, columns] = shaped[:, to]
    x_copies = []
    for d in range(1, XS):
        to = (xx + d) % XS
        copy = remote(wgs.at[to], wgr.at[d - 1], x_s.at[d - 1], x_r.at[d - 1], at(z, to, c))
        copy.start()
        x_copies.append(copy)

    def backward(query, key, value, grads, dstat, probs_ref):
        scores = []
        for h in range(2):
            grad_probs = dot_nt(grads, value * head_mask[h])
            column = dstat[:, h * E : h * E + 1]
            scores.append((probs_ref[h].astype(F32) * (grad_probs - column)).astype(BF16))
        keys = jnp.concatenate([key * head_mask[h] for h in range(2)], axis=0)
        grad_q = dot(jnp.concatenate(scores, axis=1), keys) * 0.125
        queries = jnp.concatenate([query * head_mask[h] for h in range(2)], axis=0)
        grad_k = dot_tn(jnp.concatenate(scores, axis=0), queries) * 0.125
        outs = jnp.concatenate([grads * head_mask[h] for h in range(2)], axis=0)
        grad_v = dot_tn(jnp.concatenate([probs_ref[0], probs_ref[1]], axis=0), outs)
        return grad_q, grad_k, grad_v

    acc[...] = jnp.zeros_like(acc)

    def near_backward(p, carry):
        off = offsets(0, c, p)
        grad_q, grad_k, grad_v = backward(
            qn[p].reshape(128, 128), kn[:, 0, p].reshape(T, 128), kn[:, 1, p].reshape(T, 128),
            g2[p].reshape(128, 128), d2[p].reshape(128, 128), pn.at[p],
        )
        grad_q = grad_q.reshape(2, 64, 128)
        for s in range(2):
            acc[s, 0, p] = near_spread(grad_q[s], off)
        for k, part in enumerate((grad_k, grad_v)):
            part = part.reshape(4, 64, 128)
            for s in range(2):
                acc[s, 1 + k, p] = near_spread(part[s], off)
            for r in range(2):
                nsend[r, k, p] = part[2 + r].astype(BF16)
        return carry

    lax.fori_loop(0, 2, near_backward, 0)
    near_back = []
    for r in range(2):
        copy = remote(nsend.at[r], nrecv.at[r], near_s.at[1, r], near_r.at[1, r], near_pos(r))
        copy.start()
        near_back.append(copy)

    def far_backward(p, carry):
        off = offsets(1, c, p)
        grad_q, grad_k, grad_v = backward(
            qf[p].reshape(32, 128), kf[:, 0, p].reshape(T, 128), kf[:, 1, p].reshape(T, 128),
            g3[p].reshape(32, 128), d3[p].reshape(32, 128), pf.at[p],
        )
        grad_q = grad_q.reshape(2, 16, 128)
        for s in range(2):
            acc[s, 0, p] += far_spread(grad_q[s], off)
        for k, part in enumerate((grad_k, grad_v)):
            part = part.reshape(16, 16, 128)
            for s in range(2):
                acc[s, 1 + k, p] += far_spread(part[s], off)
            fsend[:, k, p] = part[2:].astype(BF16)
        return carry

    lax.fori_loop(0, 2, far_backward, 0)
    far_back = []
    for d in range(1, 8):
        for r in range(2):
            slot = 2 * (d - 1) + r
            copy = remote(
                fsend.at[slot], frecv.at[slot],
                far_s.at[1, slot], far_r.at[1, slot], far_pos(-d, r),
            )
            copy.start()
            far_back.append(copy)

    def dense_backward(s):
        def body(p, carry):
            grad_parts = backward(
                x[s, 0, p], x[s, 1, p], x[s, 2, p], g1[s, p], d1[s, p], p1.at[s, p]
            )
            for t, part in enumerate(grad_parts):
                if s == 1:
                    sibs[t, p] = (acc[s, t, p] + part).astype(BF16)
                else:
                    acc[s, t, p] += part
            return carry

        lax.fori_loop(0, 2, body, 0)

    dense_backward(1)
    sib_back = remote(sibs, sibr, sib_s.at[2], sib_r.at[2], sib)
    sib_back.start()

    for copy in x_copies:
        copy.wait()
    total = wgs[xx].astype(F32)
    for d in range(XS - 1):
        total = total + wgr[d].astype(F32)
    for k in range(ZS):
        chunk = total[k // 2, 8 * ((k + 1) % 2) : 8 * ((k + 1) % 2) + 8]
        zsb[k] = jnp.concatenate([chunk[:, :512], chunk[:, 512:]], axis=0).astype(BF16)
    z_copies = []
    for d in range(1, ZS):
        to = (z + d) % ZS
        copy = remote(zsb.at[to], zr.at[d - 1], z_s.at[d - 1], z_r.at[d - 1], at(to, xx, c))
        copy.start()
        z_copies.append(copy)

    dense_backward(0)

    for copy in z_copies:
        copy.wait()
    total = zsb[z].astype(F32)
    for d in range(ZS - 1):
        total = total + zr[d].astype(F32)
    ysb[...] = total
    y_copies = []
    for d in range(YS):
        copy = remote(ysb, yr.at[d], y_s.at[d], y_r.at[d], y_target, (y + d) % YS)
        copy.start()
        y_copies.append(copy)

    for copy in near_back:
        copy.wait()
    for copy in far_back:
        copy.wait()

    def returned(t, p, r):
        half = c if r == 0 else 1 - c
        near = near_spread(nrecv[r, t - 1, p].astype(F32), offsets(0, half, p))
        far = frecv[r, t - 1, p].astype(F32)
        for d in range(1, 7):
            far = far + frecv[2 * d + r, t - 1, p].astype(F32)
        return near + far_spread(far, offsets(1, half, p))

    def write(t, columns, parts):
        joined = jnp.concatenate([part.astype(BF16) for part in parts], axis=1)
        out_ref[t, :, pl.ds(columns, 256)] = dot(perm[...], joined).astype(BF16)

    for t in range(3):
        parts = [acc[0, t, p] for p in range(2)]
        if t > 0:
            parts = [parts[p] + returned(t, p, 0) for p in range(2)]
        write(t, mine, parts)
    sib_back.wait()
    for t in range(3):
        parts = [sibr[t, p].astype(F32) for p in range(2)]
        if t > 0:
            parts = [parts[p] + returned(t, p, 1) for p in range(2)]
        write(t, theirs, parts)
    for copy in y_copies:
        copy.wait()
    total = ((yr[0] + yr[1]) + (yr[2] + yr[3])) * (1.0 / YS)
    wg_ref[:, :512] = total[:8]
    wg_ref[:, 512:] = total[8:]


def local(qkv, dout, out_weight, head_offsets):
    planes = jnp.transpose(qkv[0], (1, 0, 2))
    vmem = pltpu.VMEM
    dma = pltpu.SemaphoreType.DMA
    grads, weight_grad = pl.pallas_call(
        kernel,
        out_shape=(
            jax.ShapeDtypeStruct((3, T, 512), BF16),
            jax.ShapeDtypeStruct((8, 1024), F32),
        ),
        in_specs=[
            pl.BlockSpec(memory_space=pl.ANY),
            pl.BlockSpec(memory_space=pl.ANY),
            pl.BlockSpec(memory_space=pl.ANY),
            pl.BlockSpec(memory_space=pltpu.SMEM),
        ],
        out_specs=(pl.BlockSpec(memory_space=pltpu.VMEM), pl.BlockSpec(memory_space=pltpu.VMEM)),
        scratch_shapes=[
            vmem((3, T, 512), BF16),
            vmem((2, T, 1024), BF16),
            vmem((256, 1024), BF16),
            vmem((T, T), BF16),
            vmem((2, 3, 2, T, 128), BF16),
            vmem((3, 2, T, 128), BF16),
            vmem((3, 2, T, 128), BF16),
            vmem((3, 2, T, 128), BF16),
            vmem((4, 2, 2, 64, 128), BF16),
            vmem((2, 2, 64, 128), BF16),
            vmem((16, 2, 2, 16, 128), BF16),
            vmem((2, 2, 16, 128), BF16),
            vmem((2, 2, 64, 128), BF16),
            vmem((2, 2, 16, 128), BF16),
            vmem((2, 2, T, 128), BF16),
            *[vmem((2, 2, T, 128), F32)] * 3,
            *[vmem((2, 2, 64, 128), F32)] * 3,
            *[vmem((2, 2, 16, 128), F32)] * 3,
            vmem((2, 2, 2, T, T), BF16),
            vmem((2, 2, 128, T), BF16),
            vmem((2, 2, 32, T), BF16),
            vmem((2 * T, 256), BF16),
            vmem((2, 2, T, 128), BF16),
            vmem((2, 2, T, 128), F32),
            vmem((2, 2, 64, 128), BF16),
            vmem((2, 2, 64, 128), F32),
            vmem((2, 2, 16, 128), BF16),
            vmem((2, 2, 16, 128), F32),
            vmem((2, 3, 2, T, 128), F32),
            vmem((2, 2, 2, 64, 128), BF16),
            vmem((2, 2, 2, 64, 128), BF16),
            vmem((14, 2, 2, 16, 128), BF16),
            vmem((14, 2, 2, 16, 128), BF16),
            vmem((4, 4, 16, 1024), BF16),
            vmem((3, 4, 16, 1024), BF16),
            vmem((8, 16, 512), BF16),
            vmem((7, 16, 512), BF16),
            vmem((16, 512), F32),
            vmem((4, 16, 512), F32),
            dma((3,)),
            dma((3,)), dma((3,)),
            dma((2, 2)), dma((2, 2)),
            dma((2, 14)), dma((2, 14)),
            dma((3,)), dma((3,)),
            dma((7,)), dma((7,)),
            dma((4,)), dma((4,)),
        ],
        compiler_params=pltpu.CompilerParams(
            collective_id=0, has_side_effects=True, vmem_limit_bytes=48 * 1024 * 1024
        ),
        cost_estimate=pl.CostEstimate(
            flops=1_200_000_000, bytes_accessed=4_000_000, transcendentals=700_000
        ),
    )(planes, dout[0], out_weight, head_offsets)
    return jnp.transpose(grads, (1, 0, 2))[None], weight_grad


def solution(mesh):
    return jax.shard_map(
        local,
        mesh=mesh,
        in_specs=(P("dp", "seq", None, None), P("dp", "seq", None), P(), P()),
        out_specs=(P("dp", "seq", None, None), P("seq", None)),
        check_vma=False,
    )
```

```python
import jax
import jax.numpy as jnp
from jax import lax
from jax.experimental import pallas as pl
from jax.experimental.pallas import tpu as pltpu
from jax.sharding import PartitionSpec as P

XS, ZS, YS = 4, 8, 4
T = 256
E = 64
C2 = 0.125 * 1.4426950408889634
F32, BF16 = jnp.float32, jnp.bfloat16
NEG = -3.0e38


def dot(a, b):
    return lax.dot_general(a, b, (((1,), (0,)), ((), ())), preferred_element_type=F32)


def dot_nt(a, b):
    return lax.dot_general(a, b, (((1,), (1,)), ((), ())), preferred_element_type=F32)


def dot_tn(a, b):
    return lax.dot_general(a, b, (((0,), (0,)), ((), ())), preferred_element_type=F32)


def kernel(
    qkv_ref, dout_ref, w_ref, off_hbm, out_ref, wg_ref,
    qkv_in, dout2, wv, perm, x, oth, sibs, sibr, kn, ns, kf, fs, qn, qf, g,
    o1, t1, m1, o2, t2, m2, o3, t3, m3, p1, pn, pf, attn,
    g1, q1, f1s, d1, gn, g2, q2, f2s, d2, gf, g3, q3, f3s, d3,
    acc, nsend, nrecv, fsend, frecv, wgs, wgr, zsb, zr, off_ref,
    load_sem, sib_s, sib_r, near_s, near_r, far_s, far_r, xy_s, xy_r, zy_s, zy_r, known,
):
    pos = lax.axis_index("seq")
    y = lax.axis_index("dp")
    c = pos % 2
    xx = (pos // 2) % XS
    z = pos // (2 * XS)
    chip = (z % 2) * XS + xx

    def at(z_, x_, c_):
        return (z_ * XS + x_) * 2 + c_

    def far_pos(d, r):
        ch = (chip + d + 8) % 8
        return at(z - z % 2 + ch // XS, ch % XS, (c + r) % 2)

    xp = xx + 1 - 2 * (xx % 2)
    sib = at(z, xx, 1 - c)

    def near_pos(r):
        return at(z, xp, (c + r) % 2)

    z_outer = (z + 2 * (z % 2) - 1 + ZS) % ZS

    def z_pos(d):
        return at((z + d + ZS) % ZS, xx, c)

    def remote(src, dst, send, recv, target, row=None):
        where = {"seq": target} if row is None else {"seq": target, "dp": row}
        return pltpu.make_async_remote_copy(
            src_ref=src, dst_ref=dst, send_sem=send, recv_sem=recv,
            device_id=where, device_id_type=pl.DeviceIdType.MESH,
        )

    mine = pl.multiple_of(c * 256, 256)
    theirs = pl.multiple_of((1 - c) * 256, 256)
    load_qkv = pltpu.make_async_copy(qkv_ref, qkv_in, load_sem.at[0])
    load_dout = pltpu.make_async_copy(dout_ref, dout2.at[0], load_sem.at[1])
    load_w = pltpu.make_async_copy(w_ref.at[pl.ds(mine, 256), :], wv, load_sem.at[2])
    load_off = pltpu.make_async_copy(off_hbm, off_ref, load_sem.at[3])
    load_qkv.start()
    load_off.start()
    load_dout.start()
    load_w.start()

    barrier = pltpu.get_barrier_semaphore()

    def tell(semaphore, target, row=None):
        where = {"seq": target} if row is None else {"seq": target, "dp": row}
        pl.semaphore_signal(
            semaphore, inc=1, device_id=where, device_id_type=pl.DeviceIdType.MESH
        )

    tell(barrier, at(z_outer, xx, c))
    for d in range(1, YS):
        tell(barrier, pos, (y + d) % YS)
    for d in range(7, 0, -1):
        for r in range(2):
            tell(barrier, far_pos(d, r))
    tell(barrier, sib)

    lane = lax.broadcasted_iota(jnp.int32, (1, 128), 1)
    low_lane = lane < E
    head_mask = [low_lane.astype(F32).astype(BF16), (lane >= E).astype(F32).astype(BF16)]

    def offsets(row, half, pair):
        first = 4 * half + 2 * pair
        return jnp.where(low_lane, off_ref[row, first], off_ref[row, first + 1])

    def near_rows(array, off):
        shaped = array.reshape(4, 4, 16, 128)
        parts = [shaped[:, k] * (off == k).astype(F32).astype(array.dtype) for k in range(4)]
        return ((parts[0] + parts[1]) + (parts[2] + parts[3])).reshape(64, 128)

    def far_rows(array, off):
        shaped = array.reshape(16, 16, 128)
        total = shaped[0] * (off == 0).astype(F32).astype(array.dtype)
        for k in range(1, 16):
            total = total + shaped[k] * (off == k).astype(F32).astype(array.dtype)
        return total

    def near_spread(array, off):
        shaped = array.reshape(4, 1, 16, 128)
        parts = [jnp.where((off == k).reshape(1, 1, 1, 128), shaped, 0.0) for k in range(4)]
        return jnp.concatenate(parts, axis=1).reshape(T, 128)

    def far_spread(array, off):
        parts = [jnp.where(off == k, array, 0.0) for k in range(16)]
        return jnp.concatenate(parts, axis=0)

    row_id = lax.broadcasted_iota(jnp.int32, (T, T), 0)
    col_id = lax.broadcasted_iota(jnp.int32, (T, T), 1)
    swapped = (row_id % 16) * 16 + row_id // 16
    perm[...] = (swapped == col_id).astype(F32).astype(BF16)

    load_off.wait()
    load_qkv.wait()
    for t in range(3):
        own = dot(perm[...], qkv_in[t, :, pl.ds(mine, 256)]).astype(BF16)
        x[0, t, 0] = own[:, :128]
        x[0, t, 1] = own[:, 128:]
        other = dot(perm[...], qkv_in[t, :, pl.ds(theirs, 256)]).astype(BF16)
        oth[t, 0] = other[:, :128]
        oth[t, 1] = other[:, 128:]
    for p in range(2):
        near_own, far_own = offsets(0, c, p), offsets(1, c, p)
        near_other, far_other = offsets(0, 1 - c, p), offsets(1, 1 - c, p)
        for k in range(2):
            kn[0, k, p] = near_rows(x[0, 1 + k, p], near_own)
            kf[0, k, p] = far_rows(x[0, 1 + k, p], far_own)
            ns[k, p] = near_rows(oth[1 + k, p], near_other)
            fs[k, p] = far_rows(oth[1 + k, p], far_other)
        qn[p, 0] = near_rows(x[0, 0, p], near_own)
        qf[p, 0] = far_rows(x[0, 0, p], far_own)
    pl.semaphore_wait(barrier, 15 + (YS - 1) + 1)

    sib_copy = remote(oth, x.at[1], sib_s.at[0], sib_r.at[0], sib)
    sib_copy.start()
    near_copies = []
    for r in range(2):
        copy = remote(
            kn.at[0] if r == 0 else ns, kn.at[2 + r], near_s.at[0, r], near_r.at[0, r], near_pos(r)
        )
        copy.start()
        near_copies.append(copy)
    far_copies = []
    for d in range(1, 8):
        for r in range(2):
            slot = 2 * (d - 1) + r
            copy = remote(
                kf.at[0] if r == 0 else fs, kf.at[2 + slot],
                far_s.at[0, slot], far_r.at[0, slot], far_pos(d, r),
            )
            copy.start()
            far_copies.append(copy)
    load_dout.wait()
    dout_copy = remote(dout2.at[0], dout2.at[1], sib_s.at[1], sib_r.at[1], sib)
    dout_copy.start()
    for d in (-1, 1):
        tell(known.at[0], z_pos(d))

    def forward(query, key, value, probs_ref):
        probs, maxima = [], []
        for h in range(2):
            scores = dot_nt(query, key * head_mask[h])
            row_max = jnp.max(scores, axis=1, keepdims=True)
            prob = jnp.exp2((scores - row_max) * C2).astype(BF16)
            probs_ref[h] = prob
            probs.append(prob)
            maxima.append(row_max * C2)
        ones = jnp.ones((T, 128), BF16)
        right = jnp.concatenate(
            [
                jnp.concatenate([value * head_mask[h], ones * head_mask[h]], axis=1)
                for h in range(2)
            ],
            axis=0,
        )
        both = dot(jnp.concatenate(probs, axis=1), right)
        return both[:, :128], both[:, 128:], jnp.where(low_lane, maxima[0], maxima[1])

    def dense_forward(s):
        def body(p, carry):
            out, total, peak = forward(x[s, 0, p], x[s, 1, p], x[s, 2, p], p1.at[s, p])
            o1[s, p], t1[s, p], m1[s, p] = out, total, peak
            return carry

        lax.fori_loop(0, 2, body, 0)

    def grad_in(s):
        grads = dot_nt(dout2[s], wv[...]).astype(BF16)
        moved = dot(perm[...], grads).astype(BF16)
        g[s, 0] = moved[:, :128]
        g[s, 1] = moved[:, 128:]

    dense_forward(0)
    load_w.wait()
    grad_in(0)
    sib_copy.wait()
    for p in range(2):
        near_own, far_own = offsets(0, c, p), offsets(1, c, p)
        for k in range(2):
            kn[1, k, p] = near_rows(x[1, 1 + k, p], near_own)
            kf[1, k, p] = far_rows(x[1, 1 + k, p], far_own)
        qn[p, 1] = near_rows(x[1, 0, p], near_own)
        qf[p, 1] = far_rows(x[1, 0, p], far_own)
    dense_forward(1)
    pl.semaphore_wait(known.at[0], 2)
    for d in (-2, 2):
        tell(known.at[1], z_pos(d))
    dout_copy.wait()
    grad_in(1)

    for copy in near_copies:
        copy.wait()

    def near_forward(p, carry):
        out, total, peak = forward(
            qn[p].reshape(128, 128), kn[:, 0, p].reshape(T, 128), kn[:, 1, p].reshape(T, 128),
            pn.at[p],
        )
        o2[p], t2[p], m2[p] = (a.reshape(2, 64, 128) for a in (out, total, peak))
        return carry

    lax.fori_loop(0, 2, near_forward, 0)
    for copy in far_copies:
        copy.wait()
    pl.semaphore_wait(known.at[1], 2)
    tell(known.at[2], sib)

    def far_forward(p, carry):
        out, total, peak = forward(
            qf[p].reshape(32, 128), kf[:, 0, p].reshape(T, 128), kf[:, 1, p].reshape(T, 128),
            pf.at[p],
        )
        o3[p], t3[p], m3[p] = (a.reshape(2, 16, 128) for a in (out, total, peak))
        return carry

    lax.fori_loop(0, 2, far_forward, 0)

    same_head = (
        (lax.broadcasted_iota(jnp.int32, (256, 128), 0) % 128 < E)
        == (lax.broadcasted_iota(jnp.int32, (256, 128), 1) < E)
    ).astype(F32).astype(BF16)

    def combine(p, s):
        near_off, far_off = offsets(0, c, p), offsets(1, c, p)

        def near_wide(array):
            return jnp.broadcast_to(array.reshape(4, 1, 16, 128), (4, 4, 16, 128)).reshape(T, 128)

        def far_wide(array):
            return jnp.broadcast_to(array.reshape(1, 16, 128), (16, 16, 128)).reshape(T, 128)

        parts = [
            jnp.where((near_off == k).reshape(1, 1, 1, 128), m2[p, s].reshape(4, 1, 16, 128), NEG)
            for k in range(4)
        ]
        max2 = jnp.concatenate(parts, axis=1).reshape(T, 128)
        max3 = jnp.concatenate([jnp.where(far_off == k, m3[p, s], NEG) for k in range(16)], axis=0)
        max1 = m1[s, p]
        peak = jnp.maximum(jnp.maximum(max1, max2), max3)
        e1, e2, e3 = jnp.exp2(max1 - peak), jnp.exp2(max2 - peak), jnp.exp2(max3 - peak)
        denom = e1 * t1[s, p] + e2 * near_wide(t2[p, s]) + e3 * far_wide(t3[p, s])
        inverse = 1.0 / denom
        f1, f2, f3 = e1 * inverse, e2 * inverse, e3 * inverse
        mixed = f1 * o1[s, p] + f2 * near_wide(o2[p, s]) + f3 * far_wide(o3[p, s])
        low = mixed.astype(BF16)
        grads = g[s, p].astype(F32)
        query = x[s, 0, p].astype(F32)
        product = grads * low.astype(F32)
        high = product.astype(BF16)
        rest = (product - high.astype(F32)).astype(BF16)
        dstat = dot(jnp.concatenate([high, rest], axis=1), same_head)
        g1[s, p] = (grads * f1).astype(BF16)
        q1[s, p] = (query * f1).astype(BF16)
        f1s[s, p] = f1
        d1[s, p] = dstat
        near_f, near_g = near_rows(f2, near_off), near_rows(g[s, p], near_off)
        gn[p, s] = near_g
        g2[p, s] = (near_g.astype(F32) * near_f).astype(BF16)
        q2[p, s] = (qn[p, s].astype(F32) * near_f).astype(BF16)
        f2s[p, s] = near_f
        d2[p, s] = near_rows(dstat, near_off)
        far_f, far_g = far_rows(f3, far_off), far_rows(g[s, p], far_off)
        gf[p, s] = far_g
        g3[p, s] = (far_g.astype(F32) * far_f).astype(BF16)
        q3[p, s] = (qf[p, s].astype(F32) * far_f).astype(BF16)
        f3s[p, s] = far_f
        d3[p, s] = far_rows(dstat, far_off)
        return low

    for s in range(2):
        rows = jnp.concatenate([combine(p, s) for p in range(2)], axis=1)
        attn[s * T : (s + 1) * T, :] = dot(perm[...], rows).astype(BF16)

    pl.semaphore_wait(known.at[2], 1)
    for k in range(YS):
        columns = slice(256 * k, 256 * k + 256)
        both = dot_tn(attn[0:T, :], dout2[0, :, columns])
        both = both + dot_tn(attn[T:, :], dout2[1, :, columns])
        shaped = both.astype(BF16).reshape(4, XS, 16, 256)
        for to in range(XS):
            wgs[to, k] = shaped[:, to]
    xy_copies = []
    for dx in range(XS):
        for dy in range(YS):
            if dx + dy > 0:
                slot = dx * YS + dy - 1
                tx, ty = (xx + dx) % XS, (y + dy) % YS
                copy = remote(
                    wgs.at[tx, ty], wgr.at[slot], xy_s.at[slot], xy_r.at[slot], at(z, tx, c), ty
                )
                copy.start()
                xy_copies.append(copy)

    def backward(key, value, grads, dstat, factor, query_f, grads_f, probs_ref):
        scores = []
        for h in range(2):
            grad_probs = dot_nt(grads, value * head_mask[h])
            column = dstat[:, h * E : h * E + 1]
            scores.append((probs_ref[h].astype(F32) * (grad_probs - column)).astype(BF16))
        keys = jnp.concatenate([key * head_mask[h] for h in range(2)], axis=0)
        grad_q = dot(jnp.concatenate(scores, axis=1), keys) * (factor * 0.125)
        queries = jnp.concatenate([query_f * head_mask[h] for h in range(2)], axis=0)
        grad_k = dot_tn(jnp.concatenate(scores, axis=0), queries) * 0.125
        outs = jnp.concatenate([grads_f * head_mask[h] for h in range(2)], axis=0)
        grad_v = dot_tn(jnp.concatenate([probs_ref[0], probs_ref[1]], axis=0), outs)
        return grad_q, grad_k, grad_v

    def near_backward(p, carry):
        off = offsets(0, c, p)
        grad_q, grad_k, grad_v = backward(
            kn[:, 0, p].reshape(T, 128), kn[:, 1, p].reshape(T, 128),
            *(a[p].reshape(128, 128) for a in (gn, d2, f2s, q2, g2)), pn.at[p],
        )
        grad_q = grad_q.reshape(2, 64, 128)
        for s in range(2):
            acc[s, 0, p] = near_spread(grad_q[s], off)
        for k, part in enumerate((grad_k, grad_v)):
            part = part.reshape(4, 64, 128)
            for s in range(2):
                acc[s, 1 + k, p] = near_spread(part[s], off)
            for r in range(2):
                nsend[r, k, p] = part[2 + r].astype(BF16)
        return carry

    lax.fori_loop(0, 2, near_backward, 0)
    near_back = []
    for r in range(2):
        copy = remote(nsend.at[r], nrecv.at[r], near_s.at[1, r], near_r.at[1, r], near_pos(r))
        copy.start()
        near_back.append(copy)

    def far_backward(p, carry):
        off = offsets(1, c, p)
        grad_q, grad_k, grad_v = backward(
            kf[:, 0, p].reshape(T, 128), kf[:, 1, p].reshape(T, 128),
            *(a[p].reshape(32, 128) for a in (gf, d3, f3s, q3, g3)), pf.at[p],
        )
        grad_q = grad_q.reshape(2, 16, 128)
        for s in range(2):
            acc[s, 0, p] += far_spread(grad_q[s], off)
        for k, part in enumerate((grad_k, grad_v)):
            part = part.reshape(16, 16, 128)
            for s in range(2):
                acc[s, 1 + k, p] += far_spread(part[s], off)
            fsend[:, k, p] = part[2:].astype(BF16)
        return carry

    lax.fori_loop(0, 2, far_backward, 0)
    far_back = []
    for d in range(1, 8):
        for r in range(2):
            slot = 2 * (d - 1) + r
            copy = remote(
                fsend.at[slot], frecv.at[slot],
                far_s.at[1, slot], far_r.at[1, slot], far_pos(-d, r),
            )
            copy.start()
            far_back.append(copy)

    def dense_backward(s):
        def body(p, carry):
            grad_parts = backward(
                x[s, 1, p], x[s, 2, p], g[s, p], d1[s, p], f1s[s, p], q1[s, p], g1[s, p],
                p1.at[s, p],
            )
            for t, part in enumerate(grad_parts):
                if s == 1:
                    sibs[t, p] = (acc[s, t, p] + part).astype(BF16)
                else:
                    acc[s, t, p] += part
            return carry

        lax.fori_loop(0, 2, body, 0)

    dense_backward(1)
    sib_back = remote(sibs, sibr, sib_s.at[2], sib_r.at[2], sib)
    sib_back.start()

    dense_backward(0)

    for copy in xy_copies:
        copy.wait()
    total = wgs[xx, y].astype(F32)
    for d in range(XS * YS - 1):
        total = total + wgr[d].astype(F32)
    for a in range(4):
        for half in range(2):
            chunk = total[a, 8 * half : 8 * half + 8]
            zsb[a, half] = jnp.concatenate([chunk[:, :128], chunk[:, 128:]], axis=0).astype(BF16)
    zy_copies = []
    for dy in range(YS):
        for a in range(4):
            for half in range(2):
                target = at(4 * c + a, xx, half)
                source, landing = zsb.at[a, half], zr.at[dy, z]
                copy = remote(
                    source, landing, zy_s.at[dy, a, half], zy_r.at[dy, z], target, (y + dy) % YS
                )
                if dy > 0:
                    copy.start()
                else:

                    @pl.when(target != pos)
                    def _(copy=copy):
                        copy.start()

                    @pl.when(target == pos)
                    def _(source=source, landing=landing):
                        pltpu.make_async_copy(source, landing, zy_r.at[0, z]).start()

                zy_copies.append((copy, dy, target))

    for copy in near_back:
        copy.wait()
    for copy in far_back:
        copy.wait()

    def returned(t, p, r):
        half = c if r == 0 else 1 - c
        near = near_spread(nrecv[r, t - 1, p].astype(F32), offsets(0, half, p))
        far = frecv[r, t - 1, p].astype(F32)
        for d in range(1, 7):
            far = far + frecv[2 * d + r, t - 1, p].astype(F32)
        return near + far_spread(far, offsets(1, half, p))

    def write(t, columns, parts):
        joined = jnp.concatenate([part.astype(BF16) for part in parts], axis=1)
        out_ref[t, :, pl.ds(columns, 256)] = dot(perm[...], joined).astype(BF16)

    for t in range(3):
        parts = [acc[0, t, p] for p in range(2)]
        if t > 0:
            parts = [parts[p] + returned(t, p, 0) for p in range(2)]
        write(t, mine, parts)
    sib_back.wait()
    for t in range(3):
        parts = [sibr[t, p].astype(F32) for p in range(2)]
        if t > 0:
            parts = [parts[p] + returned(t, p, 1) for p in range(2)]
        write(t, theirs, parts)
    for copy, dy, target in zy_copies:
        if dy > 0:
            copy.wait_send()
        else:

            @pl.when(target != pos)
            def _(copy=copy):
                copy.wait_send()

    for dy in range(YS):
        total = jnp.zeros((16, 128), F32)
        for k in range(ZS):
            arrived = zr.at[dy, k]
            remote(arrived, arrived, zy_s.at[0, 0, 0], zy_r.at[dy, k], sib).wait_recv()
        for k in range(ZS):
            total = total + zr[dy, k].astype(F32)
        total = total * (1.0 / YS)
        first = 256 * ((y - dy + YS) % YS)
        wg_ref[:, pl.ds(pl.multiple_of(first, 128), 128)] = total[:8]
        wg_ref[:, pl.ds(pl.multiple_of(first + 128, 128), 128)] = total[8:]


def local(qkv, dout, out_weight, head_offsets):
    planes = jnp.transpose(qkv[0], (1, 0, 2))
    vmem = pltpu.VMEM
    dma = pltpu.SemaphoreType.DMA
    grads, weight_grad = pl.pallas_call(
        kernel,
        out_shape=(
            jax.ShapeDtypeStruct((3, T, 512), BF16),
            jax.ShapeDtypeStruct((8, 1024), F32),
        ),
        in_specs=[
            pl.BlockSpec(memory_space=pltpu.HBM),
            pl.BlockSpec(memory_space=pltpu.HBM),
            pl.BlockSpec(memory_space=pltpu.HBM),
            pl.BlockSpec(memory_space=pltpu.HBM),
        ],
        out_specs=(pl.BlockSpec(memory_space=pltpu.VMEM), pl.BlockSpec(memory_space=pltpu.VMEM)),
        scratch_shapes=[
            vmem((3, T, 512), BF16),
            vmem((2, T, 1024), BF16),
            vmem((256, 1024), BF16),
            vmem((T, T), BF16),
            vmem((2, 3, 2, T, 128), BF16),
            vmem((3, 2, T, 128), BF16),
            vmem((3, 2, T, 128), BF16),
            vmem((3, 2, T, 128), BF16),
            vmem((4, 2, 2, 64, 128), BF16),
            vmem((2, 2, 64, 128), BF16),
            vmem((16, 2, 2, 16, 128), BF16),
            vmem((2, 2, 16, 128), BF16),
            vmem((2, 2, 64, 128), BF16),
            vmem((2, 2, 16, 128), BF16),
            vmem((2, 2, T, 128), BF16),
            *[vmem((2, 2, T, 128), F32)] * 3,
            *[vmem((2, 2, 64, 128), F32)] * 3,
            *[vmem((2, 2, 16, 128), F32)] * 3,
            vmem((2, 2, 2, T, T), BF16),
            vmem((2, 2, 128, T), BF16),
            vmem((2, 2, 32, T), BF16),
            vmem((2 * T, 256), BF16),
            *[vmem((2, 2, T, 128), BF16)] * 2,
            *[vmem((2, 2, T, 128), F32)] * 2,
            *[vmem((2, 2, 64, 128), BF16)] * 3,
            *[vmem((2, 2, 64, 128), F32)] * 2,
            *[vmem((2, 2, 16, 128), BF16)] * 3,
            *[vmem((2, 2, 16, 128), F32)] * 2,
            vmem((2, 3, 2, T, 128), F32),
            vmem((2, 2, 2, 64, 128), BF16),
            vmem((2, 2, 2, 64, 128), BF16),
            vmem((14, 2, 2, 16, 128), BF16),
            vmem((14, 2, 2, 16, 128), BF16),
            vmem((4, 4, 4, 16, 256), BF16),
            vmem((15, 4, 16, 256), BF16),
            vmem((4, 2, 16, 128), BF16),
            vmem((4, 8, 16, 128), BF16),
            pltpu.SMEM((2, 8), jnp.int32),
            dma((4,)),
            dma((3,)), dma((3,)),
            dma((2, 2)), dma((2, 2)),
            dma((2, 14)), dma((2, 14)),
            dma((15,)), dma((15,)),
            dma((4, 4, 2)), dma((4, 8)),
            pltpu.SemaphoreType.REGULAR((3,)),
        ],
        compiler_params=pltpu.CompilerParams(
            collective_id=0, has_side_effects=True, vmem_limit_bytes=60 * 1024 * 1024
        ),
        cost_estimate=pl.CostEstimate(
            flops=1_200_000_000, bytes_accessed=4_000_000, transcendentals=700_000
        ),
    )(planes, dout[0], out_weight, head_offsets)
    return jnp.transpose(grads, (1, 0, 2))[None], weight_grad


def solution(mesh):
    return jax.shard_map(
        local,
        mesh=mesh,
        in_specs=(P("dp", "seq", None, None), P("dp", "seq", None), P(), P()),
        out_specs=(P("dp", "seq", None, None), P("seq", None)),
        check_vma=False,
    )
```

```python
import jax
import jax.numpy as jnp
from jax import lax
from jax.experimental import pallas as pl
from jax.experimental.pallas import tpu as pltpu
from jax.sharding import PartitionSpec as P

XS, ZS, YS = 4, 8, 4
T = 256
E = 64
C2 = 0.125 * 1.4426950408889634
F32, BF16 = jnp.float32, jnp.bfloat16
NEG = -3.0e38


def dot(a, b):
    return lax.dot_general(a, b, (((1,), (0,)), ((), ())), preferred_element_type=F32)


def dot_nt(a, b):
    return lax.dot_general(a, b, (((1,), (1,)), ((), ())), preferred_element_type=F32)


def dot_tn(a, b):
    return lax.dot_general(a, b, (((0,), (0,)), ((), ())), preferred_element_type=F32)


def kernel(
    qkv_ref, dout_ref, w_ref, off_hbm, out_ref, wg_ref,
    qkv_in, dout2, wv, perm, x, oth, sibs, sibr, kn, ns, kf, fs, qn, qf, g,
    o1, t1, m1, o2, t2, m2, o3, t3, m3, p1, pn, pf, attn,
    g1, q1, f1s, d1, gn, g2, q2, f2s, d2, gf, g3, q3, f3s, d3,
    acc, nsend, nrecv, fsend, frecv, wgs, wgr, zsb, zr, off_ref,
    load_sem, sib_s, sib_r, near_s, near_r, far_s, far_r, xy_s, xy_r, zy_s, zy_r, known,
):
    pos = lax.axis_index("seq")
    y = lax.axis_index("dp")
    c = pos % 2
    xx = (pos // 2) % XS
    z = pos // (2 * XS)
    chip = (z % 2) * XS + xx

    def at(z_, x_, c_):
        return (z_ * XS + x_) * 2 + c_

    def far_pos(d, r):
        ch = (chip + d + 8) % 8
        return at(z - z % 2 + ch // XS, ch % XS, (c + r) % 2)

    xp = xx + 1 - 2 * (xx % 2)
    sib = at(z, xx, 1 - c)

    def near_pos(r):
        return at(z, xp, (c + r) % 2)

    z_outer = (z + 2 * (z % 2) - 1 + ZS) % ZS

    def z_pos(d):
        return at((z + d + ZS) % ZS, xx, c)

    def remote(src, dst, send, recv, target, row=None):
        where = {"seq": target} if row is None else {"seq": target, "dp": row}
        return pltpu.make_async_remote_copy(
            src_ref=src, dst_ref=dst, send_sem=send, recv_sem=recv,
            device_id=where, device_id_type=pl.DeviceIdType.MESH,
        )

    mine = pl.multiple_of(c * 256, 256)
    theirs = pl.multiple_of((1 - c) * 256, 256)
    load_qkv = pltpu.make_async_copy(qkv_ref, qkv_in, load_sem.at[0])
    load_dout = pltpu.make_async_copy(dout_ref, dout2.at[0], load_sem.at[1])
    load_w = pltpu.make_async_copy(w_ref.at[pl.ds(mine, 256), :], wv, load_sem.at[2])
    load_off = pltpu.make_async_copy(off_hbm, off_ref, load_sem.at[3])
    load_qkv.start()
    load_off.start()
    load_dout.start()
    load_w.start()

    barrier = pltpu.get_barrier_semaphore()

    def tell(semaphore, target, row=None):
        where = {"seq": target} if row is None else {"seq": target, "dp": row}
        pl.semaphore_signal(
            semaphore, inc=1, device_id=where, device_id_type=pl.DeviceIdType.MESH
        )

    tell(barrier, at(z_outer, xx, c))
    for d in range(1, YS):
        tell(barrier, pos, (y + d) % YS)
    for d in range(7, 0, -1):
        for r in range(2):
            tell(barrier, far_pos(d, r))
    tell(barrier, sib)

    lane = lax.broadcasted_iota(jnp.int32, (1, 128), 1)
    low_lane = lane < E
    head_mask = [low_lane.astype(F32).astype(BF16), (lane >= E).astype(F32).astype(BF16)]

    def offsets(row, half, pair):
        first = 4 * half + 2 * pair
        return jnp.where(low_lane, off_ref[row, first], off_ref[row, first + 1])

    def near_rows(array, off):
        shaped = array.reshape(4, 4, 16, 128)
        parts = [shaped[:, k] * (off == k).astype(F32).astype(array.dtype) for k in range(4)]
        return ((parts[0] + parts[1]) + (parts[2] + parts[3])).reshape(64, 128)

    def far_rows(array, off):
        shaped = array.reshape(16, 16, 128)
        total = shaped[0] * (off == 0).astype(F32).astype(array.dtype)
        for k in range(1, 16):
            total = total + shaped[k] * (off == k).astype(F32).astype(array.dtype)
        return total

    def near_spread(array, off):
        shaped = array.reshape(4, 1, 16, 128)
        parts = [jnp.where((off == k).reshape(1, 1, 1, 128), shaped, 0.0) for k in range(4)]
        return jnp.concatenate(parts, axis=1).reshape(T, 128)

    def far_spread(array, off):
        parts = [jnp.where(off == k, array, 0.0) for k in range(16)]
        return jnp.concatenate(parts, axis=0)

    row_id = lax.broadcasted_iota(jnp.int32, (T, T), 0)
    col_id = lax.broadcasted_iota(jnp.int32, (T, T), 1)
    swapped = (row_id % 16) * 16 + row_id // 16
    perm[...] = (swapped == col_id).astype(F32).astype(BF16)

    load_off.wait()
    load_qkv.wait()
    for t in range(3):
        own = dot(perm[...], qkv_in[t, :, pl.ds(mine, 256)]).astype(BF16)
        x[0, t, 0] = own[:, :128]
        x[0, t, 1] = own[:, 128:]
        other = dot(perm[...], qkv_in[t, :, pl.ds(theirs, 256)]).astype(BF16)
        oth[t, 0] = other[:, :128]
        oth[t, 1] = other[:, 128:]
    for p in range(2):
        near_own, far_own = offsets(0, c, p), offsets(1, c, p)
        near_other, far_other = offsets(0, 1 - c, p), offsets(1, 1 - c, p)
        for k in range(2):
            kn[0, k, p] = near_rows(x[0, 1 + k, p], near_own)
            kf[0, k, p] = far_rows(x[0, 1 + k, p], far_own)
            ns[k, p] = near_rows(oth[1 + k, p], near_other)
            fs[k, p] = far_rows(oth[1 + k, p], far_other)
        qn[p, 0] = near_rows(x[0, 0, p], near_own)
        qf[p, 0] = far_rows(x[0, 0, p], far_own)
    pl.semaphore_wait(barrier, 15 + (YS - 1) + 1)

    sib_copy = remote(oth, x.at[1], sib_s.at[0], sib_r.at[0], sib)
    sib_copy.start()
    near_copies = []
    for r in range(2):
        copy = remote(
            kn.at[0] if r == 0 else ns, kn.at[2 + r], near_s.at[0, r], near_r.at[0, r], near_pos(r)
        )
        copy.start()
        near_copies.append(copy)
    far_copies = []
    for d in range(1, 8):
        for r in range(2):
            slot = 2 * (d - 1) + r
            copy = remote(
                kf.at[0] if r == 0 else fs, kf.at[2 + slot],
                far_s.at[0, slot], far_r.at[0, slot], far_pos(d, r),
            )
            copy.start()
            far_copies.append(copy)
    load_dout.wait()
    dout_copy = remote(dout2.at[0], dout2.at[1], sib_s.at[1], sib_r.at[1], sib)
    dout_copy.start()
    for d in (-1, 1):
        tell(known.at[0], z_pos(d))

    def forward(query, key, value, probs_ref):
        probs, maxima = [], []
        for h in range(2):
            scores = dot_nt(query, key * head_mask[h])
            row_max = jnp.max(scores, axis=1, keepdims=True)
            prob = jnp.exp2((scores - row_max) * C2).astype(BF16)
            probs_ref[h] = prob
            probs.append(prob)
            maxima.append(row_max * C2)
        ones = jnp.ones((T, 128), BF16)
        right = jnp.concatenate(
            [
                jnp.concatenate([value * head_mask[h], ones * head_mask[h]], axis=1)
                for h in range(2)
            ],
            axis=0,
        )
        both = dot(jnp.concatenate(probs, axis=1), right)
        return both[:, :128], both[:, 128:], jnp.where(low_lane, maxima[0], maxima[1])

    def dense_forward(s):
        def body(p, carry):
            out, total, peak = forward(x[s, 0, p], x[s, 1, p], x[s, 2, p], p1.at[s, p])
            o1[s, p], t1[s, p], m1[s, p] = out, total, peak
            return carry

        lax.fori_loop(0, 2, body, 0)

    def grad_in(s):
        grads = dot_nt(dout2[s], wv[...]).astype(BF16)
        moved = dot(perm[...], grads).astype(BF16)
        g[s, 0] = moved[:, :128]
        g[s, 1] = moved[:, 128:]

    dense_forward(0)
    load_w.wait()
    grad_in(0)
    sib_copy.wait()
    for p in range(2):
        near_own, far_own = offsets(0, c, p), offsets(1, c, p)
        for k in range(2):
            kn[1, k, p] = near_rows(x[1, 1 + k, p], near_own)
            kf[1, k, p] = far_rows(x[1, 1 + k, p], far_own)
        qn[p, 1] = near_rows(x[1, 0, p], near_own)
        qf[p, 1] = far_rows(x[1, 0, p], far_own)
    dense_forward(1)
    pl.semaphore_wait(known.at[0], 2)
    for d in (-2, 2):
        tell(known.at[1], z_pos(d))
    dout_copy.wait()
    grad_in(1)

    for copy in near_copies:
        copy.wait()

    def near_forward(p, carry):
        out, total, peak = forward(
            qn[p].reshape(128, 128), kn[:, 0, p].reshape(T, 128), kn[:, 1, p].reshape(T, 128),
            pn.at[p],
        )
        o2[p], t2[p], m2[p] = (a.reshape(2, 64, 128) for a in (out, total, peak))
        return carry

    lax.fori_loop(0, 2, near_forward, 0)
    for copy in far_copies:
        copy.wait()
    pl.semaphore_wait(known.at[1], 2)
    tell(known.at[2], sib)

    def far_forward(p, carry):
        out, total, peak = forward(
            qf[p].reshape(32, 128), kf[:, 0, p].reshape(T, 128), kf[:, 1, p].reshape(T, 128),
            pf.at[p],
        )
        o3[p], t3[p], m3[p] = (a.reshape(2, 16, 128) for a in (out, total, peak))
        return carry

    lax.fori_loop(0, 2, far_forward, 0)

    same_head = (
        (lax.broadcasted_iota(jnp.int32, (256, 128), 0) % 128 < E)
        == (lax.broadcasted_iota(jnp.int32, (256, 128), 1) < E)
    ).astype(F32).astype(BF16)

    def combine(p, s):
        near_off, far_off = offsets(0, c, p), offsets(1, c, p)

        def near_wide(array):
            return jnp.broadcast_to(array.reshape(4, 1, 16, 128), (4, 4, 16, 128)).reshape(T, 128)

        def far_wide(array):
            return jnp.broadcast_to(array.reshape(1, 16, 128), (16, 16, 128)).reshape(T, 128)

        parts = [
            jnp.where((near_off == k).reshape(1, 1, 1, 128), m2[p, s].reshape(4, 1, 16, 128), NEG)
            for k in range(4)
        ]
        max2 = jnp.concatenate(parts, axis=1).reshape(T, 128)
        max3 = jnp.concatenate([jnp.where(far_off == k, m3[p, s], NEG) for k in range(16)], axis=0)
        max1 = m1[s, p]
        peak = jnp.maximum(jnp.maximum(max1, max2), max3)
        e1, e2, e3 = jnp.exp2(max1 - peak), jnp.exp2(max2 - peak), jnp.exp2(max3 - peak)
        denom = e1 * t1[s, p] + e2 * near_wide(t2[p, s]) + e3 * far_wide(t3[p, s])
        inverse = 1.0 / denom
        f1, f2, f3 = e1 * inverse, e2 * inverse, e3 * inverse
        mixed = f1 * o1[s, p] + f2 * near_wide(o2[p, s]) + f3 * far_wide(o3[p, s])
        low = mixed.astype(BF16)
        grads = g[s, p].astype(F32)
        query = x[s, 0, p].astype(F32)
        product = grads * low.astype(F32)
        high = product.astype(BF16)
        rest = (product - high.astype(F32)).astype(BF16)
        dstat = dot(jnp.concatenate([high, rest], axis=1), same_head)
        g1[s, p] = (grads * f1).astype(BF16)
        q1[s, p] = (query * f1).astype(BF16)
        f1s[s, p] = f1
        d1[s, p] = dstat
        near_f, near_g = near_rows(f2, near_off), near_rows(g[s, p], near_off)
        gn[p, s] = near_g
        g2[p, s] = (near_g.astype(F32) * near_f).astype(BF16)
        q2[p, s] = (qn[p, s].astype(F32) * near_f).astype(BF16)
        f2s[p, s] = near_f
        d2[p, s] = near_rows(dstat, near_off)
        far_f, far_g = far_rows(f3, far_off), far_rows(g[s, p], far_off)
        gf[p, s] = far_g
        g3[p, s] = (far_g.astype(F32) * far_f).astype(BF16)
        q3[p, s] = (qf[p, s].astype(F32) * far_f).astype(BF16)
        f3s[p, s] = far_f
        d3[p, s] = far_rows(dstat, far_off)
        return low

    for s in range(2):
        rows = jnp.concatenate([combine(p, s) for p in range(2)], axis=1)
        attn[s * T : (s + 1) * T, :] = dot(perm[...], rows).astype(BF16)

    pl.semaphore_wait(known.at[2], 1)
    for k in range(YS):
        columns = slice(256 * k, 256 * k + 256)
        both = dot_tn(attn[0:T, :], dout2[0, :, columns])
        both = both + dot_tn(attn[T:, :], dout2[1, :, columns])
        shaped = both.astype(BF16).reshape(4, XS, 16, 256)
        for to in range(XS):
            wgs[to, k] = shaped[:, to]
    xy_copies = []
    for dx in range(XS):
        for dy in range(YS):
            if dx + dy > 0:
                slot = dx * YS + dy - 1
                tx, ty = (xx + dx) % XS, (y + dy) % YS
                copy = remote(
                    wgs.at[tx, ty], wgr.at[slot], xy_s.at[slot], xy_r.at[slot], at(z, tx, c), ty
                )
                copy.start()
                xy_copies.append(copy)

    def backward(key, value, grads, dstat, factor, query_f, grads_f, probs_ref):
        scores = []
        for h in range(2):
            grad_probs = dot_nt(grads, value * head_mask[h])
            column = dstat[:, h * E : h * E + 1]
            scores.append((probs_ref[h].astype(F32) * (grad_probs - column)).astype(BF16))
        keys = jnp.concatenate([key * head_mask[h] for h in range(2)], axis=0)
        grad_q = dot(jnp.concatenate(scores, axis=1), keys) * (factor * 0.125)
        queries = jnp.concatenate([query_f * head_mask[h] for h in range(2)], axis=0)
        grad_k = dot_tn(jnp.concatenate(scores, axis=0), queries) * 0.125
        outs = jnp.concatenate([grads_f * head_mask[h] for h in range(2)], axis=0)
        grad_v = dot_tn(jnp.concatenate([probs_ref[0], probs_ref[1]], axis=0), outs)
        return grad_q, grad_k, grad_v

    def near_backward(p, carry):
        off = offsets(0, c, p)
        grad_q, grad_k, grad_v = backward(
            kn[:, 0, p].reshape(T, 128), kn[:, 1, p].reshape(T, 128),
            *(a[p].reshape(128, 128) for a in (gn, d2, f2s, q2, g2)), pn.at[p],
        )
        grad_q = grad_q.reshape(2, 64, 128)
        for s in range(2):
            acc[s, 0, p] = near_spread(grad_q[s], off)
        for k, part in enumerate((grad_k, grad_v)):
            part = part.reshape(4, 64, 128)
            for s in range(2):
                acc[s, 1 + k, p] = near_spread(part[s], off)
            for r in range(2):
                nsend[r, k, p] = part[2 + r].astype(BF16)
        return carry

    lax.fori_loop(0, 2, near_backward, 0)
    near_back = []
    for r in range(2):
        copy = remote(nsend.at[r], nrecv.at[r], near_s.at[1, r], near_r.at[1, r], near_pos(r))
        near_back.append(copy)

    def far_backward(p, carry):
        off = offsets(1, c, p)
        grad_q, grad_k, grad_v = backward(
            kf[:, 0, p].reshape(T, 128), kf[:, 1, p].reshape(T, 128),
            *(a[p].reshape(32, 128) for a in (gf, d3, f3s, q3, g3)), pf.at[p],
        )
        grad_q = grad_q.reshape(2, 16, 128)
        for s in range(2):
            acc[s, 0, p] += far_spread(grad_q[s], off)
        for k, part in enumerate((grad_k, grad_v)):
            part = part.reshape(16, 16, 128)
            for s in range(2):
                acc[s, 1 + k, p] += far_spread(part[s], off)
            fsend[:, k, p] = part[2:].astype(BF16)
        return carry

    lax.fori_loop(0, 2, far_backward, 0)
    far_back = []
    for d in range(1, 8):
        for r in range(2):
            slot = 2 * (d - 1) + r
            copy = remote(
                fsend.at[slot], frecv.at[slot],
                far_s.at[1, slot], far_r.at[1, slot], far_pos(-d, r),
            )
            far_back.append(copy)

    def dense_backward(s):
        def body(p, carry):
            grad_parts = backward(
                x[s, 1, p], x[s, 2, p], g[s, p], d1[s, p], f1s[s, p], q1[s, p], g1[s, p],
                p1.at[s, p],
            )
            for t, part in enumerate(grad_parts):
                if s == 1:
                    sibs[t, p] = (acc[s, t, p] + part).astype(BF16)
                else:
                    acc[s, t, p] += part
            return carry

        lax.fori_loop(0, 2, body, 0)

    dense_backward(1)
    sib_back = remote(sibs, sibr, sib_s.at[2], sib_r.at[2], sib)
    sib_back.start()

    dense_backward(0)

    for copy in xy_copies:
        copy.wait_send()
    for copy in near_back + far_back:
        copy.start()
    for copy in xy_copies:
        copy.wait_recv()
    total = wgs[xx, y].astype(F32)
    for d in range(XS * YS - 1):
        total = total + wgr[d].astype(F32)
    for a in range(4):
        for half in range(2):
            chunk = total[a, 8 * half : 8 * half + 8]
            zsb[a, half] = jnp.concatenate([chunk[:, :128], chunk[:, 128:]], axis=0).astype(BF16)
    zy_copies = []
    for dy in range(YS):
        for a in range(4):
            for half in range(2):
                target = at(4 * c + a, xx, half)
                source, landing = zsb.at[a, half], zr.at[dy, z]
                copy = remote(
                    source, landing, zy_s.at[dy, a, half], zy_r.at[dy, z], target, (y + dy) % YS
                )
                if dy > 0:
                    copy.start()
                else:

                    @pl.when(target != pos)
                    def _(copy=copy):
                        copy.start()

                    @pl.when(target == pos)
                    def _(source=source, landing=landing):
                        pltpu.make_async_copy(source, landing, zy_r.at[0, z]).start()

                zy_copies.append((copy, dy, target))

    for copy in near_back:
        copy.wait()
    for copy in far_back:
        copy.wait()

    def returned(t, p, r):
        half = c if r == 0 else 1 - c
        near = near_spread(nrecv[r, t - 1, p].astype(F32), offsets(0, half, p))
        far = frecv[r, t - 1, p].astype(F32)
        for d in range(1, 7):
            far = far + frecv[2 * d + r, t - 1, p].astype(F32)
        return near + far_spread(far, offsets(1, half, p))

    def write(t, columns, parts):
        joined = jnp.concatenate([part.astype(BF16) for part in parts], axis=1)
        out_ref[t, :, pl.ds(columns, 256)] = dot(perm[...], joined).astype(BF16)

    for t in range(3):
        parts = [acc[0, t, p] for p in range(2)]
        if t > 0:
            parts = [parts[p] + returned(t, p, 0) for p in range(2)]
        write(t, mine, parts)
    sib_back.wait()
    for t in range(3):
        parts = [sibr[t, p].astype(F32) for p in range(2)]
        if t > 0:
            parts = [parts[p] + returned(t, p, 1) for p in range(2)]
        write(t, theirs, parts)
    for copy, dy, target in zy_copies:
        if dy > 0:
            copy.wait_send()
        else:

            @pl.when(target != pos)
            def _(copy=copy):
                copy.wait_send()

    for dy in range(YS):
        total = jnp.zeros((16, 128), F32)
        for k in range(ZS):
            arrived = zr.at[dy, k]
            remote(arrived, arrived, zy_s.at[0, 0, 0], zy_r.at[dy, k], sib).wait_recv()
        for k in range(ZS):
            total = total + zr[dy, k].astype(F32)
        total = total * (1.0 / YS)
        first = 256 * ((y - dy + YS) % YS)
        wg_ref[:, pl.ds(pl.multiple_of(first, 128), 128)] = total[:8]
        wg_ref[:, pl.ds(pl.multiple_of(first + 128, 128), 128)] = total[8:]


def deliver(grads_ref, weight_ref, out_ref, wg_ref, sem):
    first = pltpu.make_async_copy(grads_ref, out_ref, sem.at[0])
    second = pltpu.make_async_copy(weight_ref, wg_ref, sem.at[1])
    first.start()
    second.start()
    first.wait()
    second.wait()


def local(qkv, dout, out_weight, head_offsets):
    planes = jnp.transpose(qkv[0], (1, 0, 2))
    vmem = pltpu.VMEM
    dma = pltpu.SemaphoreType.DMA
    grads, weight_grad = pl.pallas_call(
        kernel,
        out_shape=(
            pltpu.VMEM((3, T, 512), BF16),
            pltpu.VMEM((8, 1024), F32),
        ),
        in_specs=[
            pl.BlockSpec(memory_space=pltpu.HBM),
            pl.BlockSpec(memory_space=pltpu.HBM),
            pl.BlockSpec(memory_space=pltpu.HBM),
            pl.BlockSpec(memory_space=pltpu.HBM),
        ],
        out_specs=(pl.BlockSpec(memory_space=pltpu.VMEM), pl.BlockSpec(memory_space=pltpu.VMEM)),
        scratch_shapes=[
            vmem((3, T, 512), BF16),
            vmem((2, T, 1024), BF16),
            vmem((256, 1024), BF16),
            vmem((T, T), BF16),
            vmem((2, 3, 2, T, 128), BF16),
            vmem((3, 2, T, 128), BF16),
            vmem((3, 2, T, 128), BF16),
            vmem((3, 2, T, 128), BF16),
            vmem((4, 2, 2, 64, 128), BF16),
            vmem((2, 2, 64, 128), BF16),
            vmem((16, 2, 2, 16, 128), BF16),
            vmem((2, 2, 16, 128), BF16),
            vmem((2, 2, 64, 128), BF16),
            vmem((2, 2, 16, 128), BF16),
            vmem((2, 2, T, 128), BF16),
            *[vmem((2, 2, T, 128), F32)] * 3,
            *[vmem((2, 2, 64, 128), F32)] * 3,
            *[vmem((2, 2, 16, 128), F32)] * 3,
            vmem((2, 2, 2, T, T), BF16),
            vmem((2, 2, 128, T), BF16),
            vmem((2, 2, 32, T), BF16),
            vmem((2 * T, 256), BF16),
            *[vmem((2, 2, T, 128), BF16)] * 2,
            *[vmem((2, 2, T, 128), F32)] * 2,
            *[vmem((2, 2, 64, 128), BF16)] * 3,
            *[vmem((2, 2, 64, 128), F32)] * 2,
            *[vmem((2, 2, 16, 128), BF16)] * 3,
            *[vmem((2, 2, 16, 128), F32)] * 2,
            vmem((2, 3, 2, T, 128), F32),
            vmem((2, 2, 2, 64, 128), BF16),
            vmem((2, 2, 2, 64, 128), BF16),
            vmem((14, 2, 2, 16, 128), BF16),
            vmem((14, 2, 2, 16, 128), BF16),
            vmem((4, 4, 4, 16, 256), BF16),
            vmem((15, 4, 16, 256), BF16),
            vmem((4, 2, 16, 128), BF16),
            vmem((4, 8, 16, 128), BF16),
            pltpu.SMEM((2, 8), jnp.int32),
            dma((4,)),
            dma((3,)), dma((3,)),
            dma((2, 2)), dma((2, 2)),
            dma((2, 14)), dma((2, 14)),
            dma((15,)), dma((15,)),
            dma((4, 4, 2)), dma((4, 8)),
            pltpu.SemaphoreType.REGULAR((3,)),
        ],
        compiler_params=pltpu.CompilerParams(
            collective_id=0, has_side_effects=True, vmem_limit_bytes=60 * 1024 * 1024
        ),
        cost_estimate=pl.CostEstimate(
            flops=1_200_000_000, bytes_accessed=4_000_000, transcendentals=700_000
        ),
    )(planes, dout[0], out_weight, head_offsets)
    grads, weight_grad = pl.pallas_call(
        deliver,
        out_shape=(
            jax.ShapeDtypeStruct((3, T, 512), BF16),
            jax.ShapeDtypeStruct((8, 1024), F32),
        ),
        in_specs=[pl.BlockSpec(memory_space=pl.ANY)] * 2,
        out_specs=[pl.BlockSpec(memory_space=pltpu.HBM)] * 2,
        scratch_shapes=[dma((2,))],
        compiler_params=pltpu.CompilerParams(vmem_limit_bytes=2 * 1024 * 1024),
    )(grads, weight_grad)
    return jnp.transpose(grads, (1, 0, 2))[None], weight_grad


def solution(mesh):
    return jax.shard_map(
        local,
        mesh=mesh,
        in_specs=(P("dp", "seq", None, None), P("dp", "seq", None), P(), P()),
        out_specs=(P("dp", "seq", None, None), P("seq", None)),
        check_vma=False,
    )
```

```python
import jax
import jax.numpy as jnp
from jax import lax
from jax.experimental import pallas as pl
from jax.experimental.pallas import tpu as pltpu
from jax.sharding import PartitionSpec as P

XS, ZS, YS = 4, 8, 4
T = 256
E = 64
C2 = 0.125 * 1.4426950408889634
F32, BF16 = jnp.float32, jnp.bfloat16
NEG = -3.0e38


def dot(a, b):
    return lax.dot_general(a, b, (((1,), (0,)), ((), ())), preferred_element_type=F32)


def dot_nt(a, b):
    return lax.dot_general(a, b, (((1,), (1,)), ((), ())), preferred_element_type=F32)


def dot_tn(a, b):
    return lax.dot_general(a, b, (((0,), (0,)), ((), ())), preferred_element_type=F32)


def kernel(
    qkv_ref, dout_ref, w_ref, off_hbm, out_ref, wg_ref,
    qkv_in, dout2, pdout, wv, perm, x, oth, sibs, sibr, kn, ns, kf, fs, qn, qf, g,
    o1, t1, m1, o2, t2, m2, o3, t3, m3, p1, pn, pf, attn,
    g1, q1, f1s, d1, gn, g2, q2, f2s, d2, gf, g3, q3, f3s, d3,
    acc, nsend, nrecv, fown, fsend, frecv, fback, fhome, wgs, wgr, zsb, zr, off_ref,
    load_sem, sib_s, sib_r, near_s, near_r, far_s, far_r, xy_s, xy_r, zy_s, zy_r, known,
):
    pos = lax.axis_index("seq")
    y = lax.axis_index("dp")
    c = pos % 2
    xx = (pos // 2) % XS
    z = pos // (2 * XS)

    def at(z_, x_, c_):
        return (z_ * XS + x_) * 2 + c_

    zp = z + 1 - 2 * (z % 2)

    def far_pos(dz, dx, r):
        return at(z if dz == 0 else zp, (xx + dx + XS) % XS, (c + r) % 2)

    def far_peers():
        peers = [(dz, dx, r) for dz in (1, 0) for dx in (2, 1, 3, 0) for r in (0, 1)]
        return [peer for peer in peers if peer[:2] != (0, 0)]

    xp = xx + 1 - 2 * (xx % 2)
    sib = at(z, xx, 1 - c)

    def near_pos(r):
        return at(z, xp, (c + r) % 2)

    z_outer = (z + 2 * (z % 2) - 1 + ZS) % ZS

    def z_pos(d):
        return at((z + d + ZS) % ZS, xx, c)

    def remote(src, dst, send, recv, target, row=None):
        where = {"seq": target} if row is None else {"seq": target, "dp": row}
        return pltpu.make_async_remote_copy(
            src_ref=src, dst_ref=dst, send_sem=send, recv_sem=recv,
            device_id=where, device_id_type=pl.DeviceIdType.MESH,
        )

    mine = pl.multiple_of(c * 256, 256)
    theirs = pl.multiple_of((1 - c) * 256, 256)
    load_qkv = pltpu.make_async_copy(qkv_ref, qkv_in, load_sem.at[0])
    load_dout = pltpu.make_async_copy(dout_ref, dout2.at[0], load_sem.at[1])
    load_w = pltpu.make_async_copy(w_ref.at[pl.ds(mine, 256), :], wv, load_sem.at[2])
    load_off = pltpu.make_async_copy(off_hbm, off_ref, load_sem.at[3])
    load_qkv.start()
    load_off.start()
    load_dout.start()
    load_w.start()

    barrier = pltpu.get_barrier_semaphore()

    def tell(semaphore, target, row=None):
        where = {"seq": target} if row is None else {"seq": target, "dp": row}
        pl.semaphore_signal(
            semaphore, inc=1, device_id=where, device_id_type=pl.DeviceIdType.MESH
        )

    tell(barrier, at(z_outer, xx, c))
    for d in range(1, YS):
        tell(barrier, pos, (y + d) % YS)
    for peer in far_peers():
        tell(barrier, far_pos(*peer))
    tell(barrier, sib)

    lane = lax.broadcasted_iota(jnp.int32, (1, 128), 1)
    low_lane = lane < E
    head_mask = [low_lane.astype(F32).astype(BF16), (lane >= E).astype(F32).astype(BF16)]

    def offsets(row, half, pair):
        first = 4 * half + 2 * pair
        return jnp.where(low_lane, off_ref[row, first], off_ref[row, first + 1])

    def near_rows(array, off):
        shaped = array.reshape(4, 4, 16, 128)
        parts = [shaped[:, k] * (off == k).astype(F32).astype(array.dtype) for k in range(4)]
        return ((parts[0] + parts[1]) + (parts[2] + parts[3])).reshape(64, 128)

    def far_rows(array, off):
        shaped = array.reshape(16, 16, 128)
        total = shaped[0] * (off == 0).astype(F32).astype(array.dtype)
        for k in range(1, 16):
            total = total + shaped[k] * (off == k).astype(F32).astype(array.dtype)
        return total

    def near_spread(array, off):
        shaped = array.reshape(4, 1, 16, 128)
        parts = [jnp.where((off == k).reshape(1, 1, 1, 128), shaped, 0.0) for k in range(4)]
        return jnp.concatenate(parts, axis=1).reshape(T, 128)

    def far_spread(array, off):
        parts = [jnp.where(off == k, array, 0.0) for k in range(16)]
        return jnp.concatenate(parts, axis=0)

    row_id = lax.broadcasted_iota(jnp.int32, (T, T), 0)
    col_id = lax.broadcasted_iota(jnp.int32, (T, T), 1)
    swapped = (row_id % 16) * 16 + row_id // 16
    perm[...] = (swapped == col_id).astype(F32).astype(BF16)

    load_off.wait()
    load_qkv.wait()
    for t in range(3):
        own = dot(perm[...], qkv_in[t, :, pl.ds(mine, 256)]).astype(BF16)
        x[0, t, 0] = own[:, :128]
        x[0, t, 1] = own[:, 128:]
        other = dot(perm[...], qkv_in[t, :, pl.ds(theirs, 256)]).astype(BF16)
        oth[t, 0] = other[:, :128]
        oth[t, 1] = other[:, 128:]
    for p in range(2):
        near_own, far_own = offsets(0, c, p), offsets(1, c, p)
        near_other, far_other = offsets(0, 1 - c, p), offsets(1, 1 - c, p)
        for k in range(2):
            kn[0, k, p] = near_rows(x[0, 1 + k, p], near_own)
            kf[0, k, p] = far_rows(x[0, 1 + k, p], far_own)
            ns[k, p] = near_rows(oth[1 + k, p], near_other)
            fs[k, p] = far_rows(oth[1 + k, p], far_other)
        qn[p, 0] = near_rows(x[0, 0, p], near_own)
        qf[p, 0] = far_rows(x[0, 0, p], far_own)
    pl.semaphore_wait(barrier, 15 + (YS - 1) + 1)

    far_copies = []
    for dz, dx, r in far_peers():
        slot = 8 * dz + 2 * dx + r
        copy = remote(
            kf.at[0] if r == 0 else fs, kf.at[slot],
            far_s.at[0, slot], far_r.at[0, slot], far_pos(dz, dx, r),
        )
        copy.start()
        far_copies.append(copy)
    near_copies = []
    for r in range(2):
        copy = remote(
            kn.at[0] if r == 0 else ns, kn.at[2 + r], near_s.at[0, r], near_r.at[0, r], near_pos(r)
        )
        copy.start()
        near_copies.append(copy)
    sib_copy = remote(oth, x.at[1], sib_s.at[0], sib_r.at[0], sib)
    sib_copy.start()
    load_dout.wait()
    dout_copy = remote(dout2.at[0], dout2.at[1], sib_s.at[1], sib_r.at[1], sib)
    dout_copy.start()
    for d in (-1, 1):
        tell(known.at[0], z_pos(d))

    def forward(query, key, value, probs_ref):
        probs, maxima = [], []
        for h in range(2):
            scores = dot_nt(query, key * head_mask[h])
            row_max = jnp.max(scores, axis=1, keepdims=True)
            prob = jnp.exp2((scores - row_max) * C2).astype(BF16)
            probs_ref[h] = prob
            probs.append(prob)
            maxima.append(row_max * C2)
        ones = jnp.ones((T, 128), BF16)
        right = jnp.concatenate(
            [
                jnp.concatenate([value * head_mask[h], ones * head_mask[h]], axis=1)
                for h in range(2)
            ],
            axis=0,
        )
        both = dot(jnp.concatenate(probs, axis=1), right)
        return both[:, :128], both[:, 128:], jnp.where(low_lane, maxima[0], maxima[1])

    def dense_forward(s):
        def body(p, carry):
            out, total, peak = forward(x[s, 0, p], x[s, 1, p], x[s, 2, p], p1.at[s, p])
            o1[s, p], t1[s, p], m1[s, p] = out, total, peak
            return carry

        lax.fori_loop(0, 2, body, 0)

    def grad_in(s):
        for k in range(4):
            columns = slice(256 * k, 256 * k + 256)
            pdout[s, :, columns] = dot(perm[...], dout2[s, :, columns]).astype(BF16)
        moved = dot_nt(pdout[s], wv[...]).astype(BF16)
        g[s, 0] = moved[:, :128]
        g[s, 1] = moved[:, 128:]

    dense_forward(0)
    load_w.wait()
    grad_in(0)
    sib_copy.wait()
    for p in range(2):
        near_own, far_own = offsets(0, c, p), offsets(1, c, p)
        for k in range(2):
            kn[1, k, p] = near_rows(x[1, 1 + k, p], near_own)
            kf[1, k, p] = far_rows(x[1, 1 + k, p], far_own)
        qn[p, 1] = near_rows(x[1, 0, p], near_own)
        qf[p, 1] = far_rows(x[1, 0, p], far_own)
    dense_forward(1)
    pl.semaphore_wait(known.at[0], 2)
    for d in (-2, 2):
        tell(known.at[1], z_pos(d))
    dout_copy.wait()
    grad_in(1)

    for copy in far_copies:
        copy.wait()
    pl.semaphore_wait(known.at[1], 2)
    tell(known.at[2], sib)

    def far_forward(p, carry):
        out, total, peak = forward(
            qf[p].reshape(32, 128), kf[:, 0, p].reshape(T, 128), kf[:, 1, p].reshape(T, 128),
            pf.at[p],
        )
        o3[p], t3[p], m3[p] = (a.reshape(2, 16, 128) for a in (out, total, peak))
        return carry

    for p in range(2):
        far_forward(p, 0)
    for copy in near_copies:
        copy.wait()

    def near_forward(p, carry):
        out, total, peak = forward(
            qn[p].reshape(128, 128), kn[:, 0, p].reshape(T, 128), kn[:, 1, p].reshape(T, 128),
            pn.at[p],
        )
        o2[p], t2[p], m2[p] = (a.reshape(2, 64, 128) for a in (out, total, peak))
        return carry

    for p in range(2):
        near_forward(p, 0)

    same_head = (
        (lax.broadcasted_iota(jnp.int32, (256, 128), 0) % 128 < E)
        == (lax.broadcasted_iota(jnp.int32, (256, 128), 1) < E)
    ).astype(F32).astype(BF16)

    def combine(p, s):
        near_off, far_off = offsets(0, c, p), offsets(1, c, p)

        def near_wide(array):
            return jnp.broadcast_to(array.reshape(4, 1, 16, 128), (4, 4, 16, 128)).reshape(T, 128)

        def far_wide(array):
            return jnp.broadcast_to(array.reshape(1, 16, 128), (16, 16, 128)).reshape(T, 128)

        parts = [
            jnp.where((near_off == k).reshape(1, 1, 1, 128), m2[p, s].reshape(4, 1, 16, 128), NEG)
            for k in range(4)
        ]
        max2 = jnp.concatenate(parts, axis=1).reshape(T, 128)
        max3 = jnp.concatenate([jnp.where(far_off == k, m3[p, s], NEG) for k in range(16)], axis=0)
        max1 = m1[s, p]
        peak = jnp.maximum(jnp.maximum(max1, max2), max3)
        e1, e2, e3 = jnp.exp2(max1 - peak), jnp.exp2(max2 - peak), jnp.exp2(max3 - peak)
        denom = e1 * t1[s, p] + e2 * near_wide(t2[p, s]) + e3 * far_wide(t3[p, s])
        inverse = 1.0 / denom
        f1, f2, f3 = e1 * inverse, e2 * inverse, e3 * inverse
        mixed = f1 * o1[s, p] + f2 * near_wide(o2[p, s]) + f3 * far_wide(o3[p, s])
        low = mixed.astype(BF16)
        grads = g[s, p].astype(F32)
        query = x[s, 0, p].astype(F32)
        product = grads * low.astype(F32)
        high = product.astype(BF16)
        rest = (product - high.astype(F32)).astype(BF16)
        dstat = dot(jnp.concatenate([high, rest], axis=1), same_head)
        g1[s, p] = (grads * f1).astype(BF16)
        q1[s, p] = (query * f1).astype(BF16)
        f1s[s, p] = f1
        d1[s, p] = dstat
        near_f, near_g = near_rows(f2, near_off), near_rows(g[s, p], near_off)
        gn[p, s] = near_g
        g2[p, s] = (near_g.astype(F32) * near_f).astype(BF16)
        q2[p, s] = (qn[p, s].astype(F32) * near_f).astype(BF16)
        f2s[p, s] = near_f
        d2[p, s] = near_rows(dstat, near_off)
        far_f, far_g = far_rows(f3, far_off), far_rows(g[s, p], far_off)
        gf[p, s] = far_g
        g3[p, s] = (far_g.astype(F32) * far_f).astype(BF16)
        q3[p, s] = (qf[p, s].astype(F32) * far_f).astype(BF16)
        f3s[p, s] = far_f
        d3[p, s] = far_rows(dstat, far_off)
        return low

    for s in range(2):
        rows = jnp.concatenate([combine(p, s) for p in range(2)], axis=1)
        attn[s * T : (s + 1) * T, :] = rows

    pl.semaphore_wait(known.at[2], 1)
    xy_copies = []
    for dy in (2, 1, 3, 0):
        ty = (y + dy) % YS
        columns = pl.ds(pl.multiple_of(256 * ty, 256), 256)
        both = dot_tn(attn[0:T, :], pdout[0, :, columns])
        both = both + dot_tn(attn[T:, :], pdout[1, :, columns])
        shaped = both.astype(BF16).reshape(4, XS, 16, 256)
        for to in range(XS):
            wgs[dy, to] = shaped[:, to]
        for dx in (2, 1, 3, 0):
            if dx + dy > 0:
                slot = dx * YS + dy - 1
                tx = (xx + dx) % XS
                copy = remote(
                    wgs.at[dy, tx], wgr.at[slot], xy_s.at[slot], xy_r.at[slot], at(z, tx, c), ty
                )
                copy.start()
                xy_copies.append((slot, copy))

    def backward(key, value, grads, dstat, factor, query_f, grads_f, probs_ref):
        scores = []
        for h in range(2):
            grad_probs = dot_nt(grads, value * head_mask[h])
            column = dstat[:, h * E : h * E + 1]
            scores.append((probs_ref[h].astype(F32) * (grad_probs - column)).astype(BF16))
        keys = jnp.concatenate([key * head_mask[h] for h in range(2)], axis=0)
        grad_q = dot(jnp.concatenate(scores, axis=1), keys) * (factor * 0.125)
        queries = jnp.concatenate([query_f * head_mask[h] for h in range(2)], axis=0)
        grad_k = dot_tn(jnp.concatenate(scores, axis=0), queries) * 0.125
        outs = jnp.concatenate([grads_f * head_mask[h] for h in range(2)], axis=0)
        grad_v = dot_tn(jnp.concatenate([probs_ref[0], probs_ref[1]], axis=0), outs)
        return grad_q, grad_k, grad_v

    def near_backward(p, carry):
        off = offsets(0, c, p)
        grad_q, grad_k, grad_v = backward(
            kn[:, 0, p].reshape(T, 128), kn[:, 1, p].reshape(T, 128),
            *(a[p].reshape(128, 128) for a in (gn, d2, f2s, q2, g2)), pn.at[p],
        )
        grad_q = grad_q.reshape(2, 64, 128)
        for s in range(2):
            acc[s, 0, p] = near_spread(grad_q[s], off)
        for k, part in enumerate((grad_k, grad_v)):
            part = part.reshape(4, 64, 128)
            for s in range(2):
                acc[s, 1 + k, p] = near_spread(part[s], off)
            for r in range(2):
                nsend[r, k, p] = part[2 + r].astype(BF16)
        return carry

    lax.fori_loop(0, 2, near_backward, 0)
    near_back = []
    for r in range(2):
        copy = remote(nsend.at[r], nrecv.at[r], near_s.at[1, r], near_r.at[1, r], near_pos(r))
        near_back.append(copy)

    def far_backward(p, carry):
        off = offsets(1, c, p)
        grad_q, grad_k, grad_v = backward(
            kf[:, 0, p].reshape(T, 128), kf[:, 1, p].reshape(T, 128),
            *(a[p].reshape(32, 128) for a in (gf, d3, f3s, q3, g3)), pf.at[p],
        )
        grad_q = grad_q.reshape(2, 16, 128)
        for s in range(2):
            acc[s, 0, p] += far_spread(grad_q[s], off)
        for k, part in enumerate((grad_k, grad_v)):
            part = part.reshape(16, 16, 128)
            fown[:, k, p] = part[:8]
            fsend[:, k, p] = part[8:].astype(BF16)
        return carry

    lax.fori_loop(0, 2, far_backward, 0)
    plane_back = remote(fsend, frecv, far_s.at[1, 0], far_r.at[1, 0], at(zp, xx, c))
    plane_back.start()

    def dense_backward(s):
        def body(p, carry):
            grad_parts = backward(
                x[s, 1, p], x[s, 2, p], g[s, p], d1[s, p], f1s[s, p], q1[s, p], g1[s, p],
                p1.at[s, p],
            )
            for t, part in enumerate(grad_parts):
                acc[s, t, p] += part
            return carry

        lax.fori_loop(0, 2, body, 0)

    dense_backward(1)
    plane_back.wait()
    for k in range(2):
        for p in range(2):
            off = offsets(1, c, p)
            both = fown[:, k, p] + frecv[:, k, p].astype(F32)
            for s in range(2):
                acc[s, 1 + k, p] += far_spread(both[s], off)
            fback[:, k, p] = both[2:].astype(BF16)
    sibs[...] = acc[1].astype(BF16)
    sib_back = remote(sibs, sibr, sib_s.at[2], sib_r.at[2], sib)
    sib_back.start()
    far_back = []
    for dx in (2, 1, 3):
        for r in range(2):
            slot = 2 * (dx - 1) + r
            copy = remote(
                fback.at[slot], fhome.at[slot], far_s.at[1, 8 + slot], far_r.at[1, 8 + slot],
                far_pos(0, -dx, r),
            )
            far_back.append(copy)

    dense_backward(0)

    for _, copy in xy_copies:
        copy.wait_send()
    for copy in near_back + far_back:
        copy.start()
    total = wgs[0, xx].astype(F32)
    for slot, copy in reversed(xy_copies):
        copy.wait_recv()
        total = total + wgr[slot].astype(F32)
    for a in range(4):
        for half in range(2):
            chunk = total[a, 8 * half : 8 * half + 8]
            zsb[a, half] = jnp.concatenate([chunk[:, :128], chunk[:, 128:]], axis=0).astype(BF16)
    zy_copies = []
    for dy in (2, 1, 3, 0):
        for a in range(4):
            for half in range(2):
                target = at(4 * c + a, xx, half)
                source, landing = zsb.at[a, half], zr.at[dy, z]
                copy = remote(
                    source, landing, zy_s.at[dy, a, half], zy_r.at[dy, z], target, (y + dy) % YS
                )
                if dy > 0:
                    copy.start()
                else:

                    @pl.when(target != pos)
                    def _(copy=copy):
                        copy.start()

                    @pl.when(target == pos)
                    def _(source=source, landing=landing):
                        pltpu.make_async_copy(source, landing, zy_r.at[0, z]).start()

                zy_copies.append((copy, dy, target))

    for copy in near_back:
        copy.wait()
    for copy in far_back:
        copy.wait()

    def returned(t, p, r):
        half = c if r == 0 else 1 - c
        near = near_spread(nrecv[r, t - 1, p].astype(F32), offsets(0, half, p))
        far = fhome[r, t - 1, p].astype(F32)
        for d in range(1, 3):
            far = far + fhome[2 * d + r, t - 1, p].astype(F32)
        return near + far_spread(far, offsets(1, half, p))

    def write(t, columns, parts):
        joined = jnp.concatenate([part.astype(BF16) for part in parts], axis=1)
        out_ref[t, :, pl.ds(columns, 256)] = dot(perm[...], joined).astype(BF16)

    for t in range(3):
        parts = [acc[0, t, p] for p in range(2)]
        if t > 0:
            parts = [parts[p] + returned(t, p, 0) for p in range(2)]
        write(t, mine, parts)
    sib_back.wait()
    for t in range(3):
        parts = [sibr[t, p].astype(F32) for p in range(2)]
        if t > 0:
            parts = [parts[p] + returned(t, p, 1) for p in range(2)]
        write(t, theirs, parts)
    for copy, dy, target in zy_copies:
        if dy > 0:
            copy.wait_send()
        else:

            @pl.when(target != pos)
            def _(copy=copy):
                copy.wait_send()

    for dy in range(YS):
        total = jnp.zeros((16, 128), F32)
        for k in range(ZS):
            arrived = zr.at[dy, k]
            remote(arrived, arrived, zy_s.at[0, 0, 0], zy_r.at[dy, k], sib).wait_recv()
            total = total + zr[dy, k].astype(F32)
        total = total * (1.0 / YS)
        first = 256 * ((y - dy + YS) % YS)
        wg_ref[:, pl.ds(pl.multiple_of(first, 128), 128)] = total[:8]
        wg_ref[:, pl.ds(pl.multiple_of(first + 128, 128), 128)] = total[8:]


def deliver(grads_ref, weight_ref, out_ref, wg_ref, sem):
    first = pltpu.make_async_copy(grads_ref, out_ref, sem.at[0])
    second = pltpu.make_async_copy(weight_ref, wg_ref, sem.at[1])
    first.start()
    second.start()
    first.wait()
    second.wait()


def local(qkv, dout, out_weight, head_offsets):
    planes = jnp.transpose(qkv[0], (1, 0, 2))
    vmem = pltpu.VMEM
    dma = pltpu.SemaphoreType.DMA
    grads, weight_grad = pl.pallas_call(
        kernel,
        out_shape=(
            pltpu.VMEM((3, T, 512), BF16),
            pltpu.VMEM((8, 1024), F32),
        ),
        in_specs=[
            pl.BlockSpec(memory_space=pltpu.HBM),
            pl.BlockSpec(memory_space=pltpu.HBM),
            pl.BlockSpec(memory_space=pltpu.HBM),
            pl.BlockSpec(memory_space=pltpu.HBM),
        ],
        out_specs=(pl.BlockSpec(memory_space=pltpu.VMEM), pl.BlockSpec(memory_space=pltpu.VMEM)),
        scratch_shapes=[
            vmem((3, T, 512), BF16),
            *[vmem((2, T, 1024), BF16)] * 2,
            vmem((256, 1024), BF16),
            vmem((T, T), BF16),
            vmem((2, 3, 2, T, 128), BF16),
            vmem((3, 2, T, 128), BF16),
            vmem((3, 2, T, 128), BF16),
            vmem((3, 2, T, 128), BF16),
            vmem((4, 2, 2, 64, 128), BF16),
            vmem((2, 2, 64, 128), BF16),
            vmem((16, 2, 2, 16, 128), BF16),
            vmem((2, 2, 16, 128), BF16),
            vmem((2, 2, 64, 128), BF16),
            vmem((2, 2, 16, 128), BF16),
            vmem((2, 2, T, 128), BF16),
            *[vmem((2, 2, T, 128), F32)] * 3,
            *[vmem((2, 2, 64, 128), F32)] * 3,
            *[vmem((2, 2, 16, 128), F32)] * 3,
            vmem((2, 2, 2, T, T), BF16),
            vmem((2, 2, 128, T), BF16),
            vmem((2, 2, 32, T), BF16),
            vmem((2 * T, 256), BF16),
            *[vmem((2, 2, T, 128), BF16)] * 2,
            *[vmem((2, 2, T, 128), F32)] * 2,
            *[vmem((2, 2, 64, 128), BF16)] * 3,
            *[vmem((2, 2, 64, 128), F32)] * 2,
            *[vmem((2, 2, 16, 128), BF16)] * 3,
            *[vmem((2, 2, 16, 128), F32)] * 2,
            vmem((2, 3, 2, T, 128), F32),
            vmem((2, 2, 2, 64, 128), BF16),
            vmem((2, 2, 2, 64, 128), BF16),
            vmem((8, 2, 2, 16, 128), F32),
            *[vmem((8, 2, 2, 16, 128), BF16)] * 2,
            *[vmem((6, 2, 2, 16, 128), BF16)] * 2,
            vmem((4, 4, 4, 16, 256), BF16),
            vmem((15, 4, 16, 256), BF16),
            vmem((4, 2, 16, 128), BF16),
            vmem((4, 8, 16, 128), BF16),
            pltpu.SMEM((2, 8), jnp.int32),
            dma((4,)),
            dma((3,)), dma((3,)),
            dma((2, 2)), dma((2, 2)),
            dma((2, 16)), dma((2, 16)),
            dma((15,)), dma((15,)),
            dma((4, 4, 2)), dma((4, 8)),
            pltpu.SemaphoreType.REGULAR((3,)),
        ],
        compiler_params=pltpu.CompilerParams(
            collective_id=0, has_side_effects=True, vmem_limit_bytes=60 * 1024 * 1024
        ),
        cost_estimate=pl.CostEstimate(
            flops=1_200_000_000, bytes_accessed=4_000_000, transcendentals=700_000
        ),
    )(planes, dout[0], out_weight, head_offsets)
    grads, weight_grad = pl.pallas_call(
        deliver,
        out_shape=(
            jax.ShapeDtypeStruct((3, T, 512), BF16),
            jax.ShapeDtypeStruct((8, 1024), F32),
        ),
        in_specs=[pl.BlockSpec(memory_space=pl.ANY)] * 2,
        out_specs=[pl.BlockSpec(memory_space=pltpu.HBM)] * 2,
        scratch_shapes=[dma((2,))],
        compiler_params=pltpu.CompilerParams(vmem_limit_bytes=2 * 1024 * 1024),
    )(grads, weight_grad)
    return jnp.transpose(grads, (1, 0, 2))[None], weight_grad


def solution(mesh):
    return jax.shard_map(
        local,
        mesh=mesh,
        in_specs=(P("dp", "seq", None, None), P("dp", "seq", None), P(), P()),
        out_specs=(P("dp", "seq", None, None), P("seq", None)),
        check_vma=False,
    )
```

```python
import jax
import jax.numpy as jnp
from jax import lax
from jax.experimental import pallas as pl
from jax.experimental.pallas import tpu as pltpu
from jax.sharding import PartitionSpec as P

XS, ZS, YS = 4, 8, 4
T = 256
E = 64
C2 = 0.125 * 1.4426950408889634
F32, BF16 = jnp.float32, jnp.bfloat16
NEG = -3.0e38


def dot(a, b):
    return lax.dot_general(a, b, (((1,), (0,)), ((), ())), preferred_element_type=F32)


def dot_nt(a, b):
    return lax.dot_general(a, b, (((1,), (1,)), ((), ())), preferred_element_type=F32)


def dot_tn(a, b):
    return lax.dot_general(a, b, (((0,), (0,)), ((), ())), preferred_element_type=F32)


def kernel(
    qkv_ref, dout_ref, w_ref, off_hbm, out_ref, wg_ref,
    qkv_in, dout2, pdout, wv, perm, x, oth, sibs, sibr, kn, ns, kf, fs, qn, qf, g,
    o1, t1, m1, o2, t2, m2, o3, t3, m3, p1, pn, pf, attn,
    g1, q1, f1s, d1, gn, g2, q2, f2s, d2, gf, g3, q3, f3s, d3,
    acc, nsend, nrecv, fown, fsend, frecv, fback, fhome, wgs, wgr, zsb, zr, off_ref,
    load_sem, sib_s, sib_r, near_s, near_r, far_s, far_r, xy_s, xy_r, zy_s, zy_r, known,
):
    pos = lax.axis_index("seq")
    y = lax.axis_index("dp")
    c = pos % 2
    xx = (pos // 2) % XS
    z = pos // (2 * XS)

    def at(z_, x_, c_):
        return (z_ * XS + x_) * 2 + c_

    zp = z + 1 - 2 * (z % 2)

    def far_pos(dz, dx, r):
        return at(z if dz == 0 else zp, (xx + dx + XS) % XS, (c + r) % 2)

    def far_peers():
        peers = [(dz, dx, r) for dz in (1, 0) for dx in (2, 1, 3, 0) for r in (0, 1)]
        return [peer for peer in peers if peer[:2] != (0, 0)]

    xp = xx + 1 - 2 * (xx % 2)
    sib = at(z, xx, 1 - c)

    def near_pos(r):
        return at(z, xp, (c + r) % 2)

    z_outer = (z + 2 * (z % 2) - 1 + ZS) % ZS

    def z_pos(d):
        return at((z + d + ZS) % ZS, xx, c)

    def remote(src, dst, send, recv, target, row=None):
        where = {"seq": target} if row is None else {"seq": target, "dp": row}
        return pltpu.make_async_remote_copy(
            src_ref=src, dst_ref=dst, send_sem=send, recv_sem=recv,
            device_id=where, device_id_type=pl.DeviceIdType.MESH,
        )

    mine = pl.multiple_of(c * 256, 256)
    theirs = pl.multiple_of((1 - c) * 256, 256)
    load_qkv = pltpu.make_async_copy(qkv_ref, qkv_in, load_sem.at[0])
    load_dout = pltpu.make_async_copy(dout_ref, dout2.at[0], load_sem.at[1])
    load_w = pltpu.make_async_copy(w_ref.at[pl.ds(mine, 256), :], wv, load_sem.at[2])
    load_off = pltpu.make_async_copy(off_hbm, off_ref, load_sem.at[3])
    load_qkv.start()
    load_off.start()
    load_dout.start()
    load_w.start()

    barrier = pltpu.get_barrier_semaphore()

    def tell(semaphore, target, row=None):
        where = {"seq": target} if row is None else {"seq": target, "dp": row}
        pl.semaphore_signal(
            semaphore, inc=1, device_id=where, device_id_type=pl.DeviceIdType.MESH
        )

    tell(barrier, at(z_outer, xx, c))
    for d in range(1, YS):
        tell(barrier, pos, (y + d) % YS)
    for peer in far_peers():
        tell(barrier, far_pos(*peer))
    tell(barrier, sib)

    lane = lax.broadcasted_iota(jnp.int32, (1, 128), 1)
    low_lane = lane < E
    head_mask = [low_lane.astype(F32).astype(BF16), (lane >= E).astype(F32).astype(BF16)]

    def offsets(row, half, pair):
        first = 4 * half + 2 * pair
        return jnp.where(low_lane, off_ref[row, first], off_ref[row, first + 1])

    def near_rows(array, off):
        shaped = array.reshape(4, 4, 16, 128)
        parts = [shaped[:, k] * (off == k).astype(F32).astype(array.dtype) for k in range(4)]
        return ((parts[0] + parts[1]) + (parts[2] + parts[3])).reshape(64, 128)

    def far_rows(array, off):
        shaped = array.reshape(16, 16, 128)
        total = shaped[0] * (off == 0).astype(F32).astype(array.dtype)
        for k in range(1, 16):
            total = total + shaped[k] * (off == k).astype(F32).astype(array.dtype)
        return total

    def near_spread(array, off):
        shaped = array.reshape(4, 1, 16, 128)
        parts = [jnp.where((off == k).reshape(1, 1, 1, 128), shaped, 0.0) for k in range(4)]
        return jnp.concatenate(parts, axis=1).reshape(T, 128)

    def far_spread(array, off):
        parts = [jnp.where(off == k, array, 0.0) for k in range(16)]
        return jnp.concatenate(parts, axis=0)

    row_id = lax.broadcasted_iota(jnp.int32, (T, T), 0)
    col_id = lax.broadcasted_iota(jnp.int32, (T, T), 1)
    swapped = (row_id % 16) * 16 + row_id // 16
    perm[...] = (swapped == col_id).astype(F32).astype(BF16)

    load_off.wait()
    load_qkv.wait()
    for t in range(3):
        own = dot(perm[...], qkv_in[t, :, pl.ds(mine, 256)]).astype(BF16)
        x[0, t, 0] = own[:, :128]
        x[0, t, 1] = own[:, 128:]
        other = dot(perm[...], qkv_in[t, :, pl.ds(theirs, 256)]).astype(BF16)
        oth[t, 0] = other[:, :128]
        oth[t, 1] = other[:, 128:]
    for p in range(2):
        near_own, far_own = offsets(0, c, p), offsets(1, c, p)
        near_other, far_other = offsets(0, 1 - c, p), offsets(1, 1 - c, p)
        for k in range(2):
            kn[0, k, p] = near_rows(x[0, 1 + k, p], near_own)
            kf[0, k, p] = far_rows(x[0, 1 + k, p], far_own)
            ns[k, p] = near_rows(oth[1 + k, p], near_other)
            fs[k, p] = far_rows(oth[1 + k, p], far_other)
        qn[p, 0] = near_rows(x[0, 0, p], near_own)
        qf[p, 0] = far_rows(x[0, 0, p], far_own)
    pl.semaphore_wait(barrier, 15 + (YS - 1) + 1)

    far_copies = []
    for dz, dx, r in far_peers():
        slot = 8 * dz + 2 * dx + r
        copy = remote(
            kf.at[0] if r == 0 else fs, kf.at[slot],
            far_s.at[0, slot], far_r.at[0, slot], far_pos(dz, dx, r),
        )
        copy.start()
        far_copies.append(copy)
    near_copies = []
    for r in range(2):
        copy = remote(
            kn.at[0] if r == 0 else ns, kn.at[2 + r], near_s.at[0, r], near_r.at[0, r], near_pos(r)
        )
        copy.start()
        near_copies.append(copy)
    sib_copy = remote(oth, x.at[1], sib_s.at[0], sib_r.at[0], sib)
    sib_copy.start()
    load_dout.wait()
    dout_copy = remote(dout2.at[0], dout2.at[1], sib_s.at[1], sib_r.at[1], sib)
    dout_copy.start()
    for d in (-1, 1):
        tell(known.at[0], z_pos(d))

    def forward(query, key, value, probs_ref):
        probs, maxima = [], []
        for h in range(2):
            scores = dot_nt(query, key * head_mask[h])
            row_max = jnp.max(scores, axis=1, keepdims=True)
            prob = jnp.exp2((scores - row_max) * C2).astype(BF16)
            probs_ref[h] = prob
            probs.append(prob)
            maxima.append(row_max * C2)
        ones = jnp.ones((T, 128), BF16)
        right = jnp.concatenate(
            [
                jnp.concatenate([value * head_mask[h], ones * head_mask[h]], axis=1)
                for h in range(2)
            ],
            axis=0,
        )
        both = dot(jnp.concatenate(probs, axis=1), right)
        return both[:, :128], both[:, 128:], jnp.where(low_lane, maxima[0], maxima[1])

    def dense_forward(s):
        def body(p, carry):
            out, total, peak = forward(x[s, 0, p], x[s, 1, p], x[s, 2, p], p1.at[s, p])
            o1[s, p], t1[s, p], m1[s, p] = out, total, peak
            return carry

        for p in range(2):
            body(p, 0)

    def grad_in(s):
        for k in range(4):
            columns = slice(256 * k, 256 * k + 256)
            pdout[s, :, columns] = dot(perm[...], dout2[s, :, columns]).astype(BF16)
        moved = dot_nt(pdout[s], wv[...]).astype(BF16)
        g[s, 0] = moved[:, :128]
        g[s, 1] = moved[:, 128:]

    dense_forward(0)
    load_w.wait()
    grad_in(0)
    sib_copy.wait()
    for p in range(2):
        near_own, far_own = offsets(0, c, p), offsets(1, c, p)
        for k in range(2):
            kn[1, k, p] = near_rows(x[1, 1 + k, p], near_own)
            kf[1, k, p] = far_rows(x[1, 1 + k, p], far_own)
        qn[p, 1] = near_rows(x[1, 0, p], near_own)
        qf[p, 1] = far_rows(x[1, 0, p], far_own)
    dense_forward(1)
    pl.semaphore_wait(known.at[0], 2)
    for d in (-2, 2):
        tell(known.at[1], z_pos(d))
    dout_copy.wait()
    grad_in(1)

    for copy in far_copies:
        copy.wait()
    pl.semaphore_wait(known.at[1], 2)
    tell(known.at[2], sib)

    def far_forward(p, carry):
        out, total, peak = forward(
            qf[p].reshape(32, 128), kf[:, 0, p].reshape(T, 128), kf[:, 1, p].reshape(T, 128),
            pf.at[p],
        )
        o3[p], t3[p], m3[p] = (a.reshape(2, 16, 128) for a in (out, total, peak))
        return carry

    for p in range(2):
        far_forward(p, 0)
    for copy in near_copies:
        copy.wait()

    def near_forward(p, carry):
        out, total, peak = forward(
            qn[p].reshape(128, 128), kn[:, 0, p].reshape(T, 128), kn[:, 1, p].reshape(T, 128),
            pn.at[p],
        )
        o2[p], t2[p], m2[p] = (a.reshape(2, 64, 128) for a in (out, total, peak))
        return carry

    for p in range(2):
        near_forward(p, 0)

    same_head = (
        (lax.broadcasted_iota(jnp.int32, (256, 128), 0) % 128 < E)
        == (lax.broadcasted_iota(jnp.int32, (256, 128), 1) < E)
    ).astype(F32).astype(BF16)

    def combine(p, s):
        near_off, far_off = offsets(0, c, p), offsets(1, c, p)

        def near_wide(array):
            return jnp.broadcast_to(array.reshape(4, 1, 16, 128), (4, 4, 16, 128)).reshape(T, 128)

        def far_wide(array):
            return jnp.broadcast_to(array.reshape(1, 16, 128), (16, 16, 128)).reshape(T, 128)

        parts = [
            jnp.where((near_off == k).reshape(1, 1, 1, 128), m2[p, s].reshape(4, 1, 16, 128), NEG)
            for k in range(4)
        ]
        max2 = jnp.concatenate(parts, axis=1).reshape(T, 128)
        max3 = jnp.concatenate([jnp.where(far_off == k, m3[p, s], NEG) for k in range(16)], axis=0)
        max1 = m1[s, p]
        peak = jnp.maximum(jnp.maximum(max1, max2), max3)
        e1, e2, e3 = jnp.exp2(max1 - peak), jnp.exp2(max2 - peak), jnp.exp2(max3 - peak)
        denom = e1 * t1[s, p] + e2 * near_wide(t2[p, s]) + e3 * far_wide(t3[p, s])
        inverse = 1.0 / denom
        f1, f2, f3 = e1 * inverse, e2 * inverse, e3 * inverse
        mixed = f1 * o1[s, p] + f2 * near_wide(o2[p, s]) + f3 * far_wide(o3[p, s])
        low = mixed.astype(BF16)
        grads = g[s, p].astype(F32)
        query = x[s, 0, p].astype(F32)
        product = grads * low.astype(F32)
        high = product.astype(BF16)
        rest = (product - high.astype(F32)).astype(BF16)
        dstat = dot(jnp.concatenate([high, rest], axis=1), same_head)
        g1[s, p] = (grads * f1).astype(BF16)
        q1[s, p] = (query * f1).astype(BF16)
        f1s[s, p] = f1
        d1[s, p] = dstat
        near_f, near_g = near_rows(f2, near_off), near_rows(g[s, p], near_off)
        gn[p, s] = near_g
        g2[p, s] = (near_g.astype(F32) * near_f).astype(BF16)
        q2[p, s] = (qn[p, s].astype(F32) * near_f).astype(BF16)
        f2s[p, s] = near_f
        d2[p, s] = near_rows(dstat, near_off)
        far_f, far_g = far_rows(f3, far_off), far_rows(g[s, p], far_off)
        gf[p, s] = far_g
        g3[p, s] = (far_g.astype(F32) * far_f).astype(BF16)
        q3[p, s] = (qf[p, s].astype(F32) * far_f).astype(BF16)
        f3s[p, s] = far_f
        d3[p, s] = far_rows(dstat, far_off)
        return low

    for s in range(2):
        for p in range(2):
            attn[128 * p : 128 * p + 128, s * T : (s + 1) * T] = jnp.transpose(combine(p, s))

    pl.semaphore_wait(known.at[2], 1)
    xy_copies = []
    for dy in (2, 1, 3, 0):
        ty = (y + dy) % YS
        columns = pl.ds(pl.multiple_of(256 * ty, 256), 256)
        both = dot(attn[...], pdout[:, :, columns].reshape(2 * T, 256))
        shaped = both.astype(BF16).reshape(4, XS, 16, 256)
        for to in range(XS):
            wgs[dy, to] = shaped[:, to]
    for dx, dy in ((2, 2), (2, 1), (2, 3), (1, 2), (3, 2), (2, 0), (0, 2), (1, 1), (1, 3), (3, 1),
                   (3, 3), (1, 0), (3, 0), (0, 1), (0, 3)):
        slot = dx * YS + dy - 1
        tx, ty = (xx + dx) % XS, (y + dy) % YS
        copy = remote(wgs.at[dy, tx], wgr.at[slot], xy_s.at[slot], xy_r.at[slot], at(z, tx, c), ty)
        copy.start()
        xy_copies.append((slot, copy))

    def backward(key, value, grads, dstat, factor, query_f, grads_f, probs_ref):
        scores = []
        for h in range(2):
            grad_probs = dot_nt(grads, value * head_mask[h])
            column = dstat[:, h * E : h * E + 1]
            scores.append((probs_ref[h].astype(F32) * (grad_probs - column)).astype(BF16))
        keys = jnp.concatenate([key * head_mask[h] for h in range(2)], axis=0)
        grad_q = dot(jnp.concatenate(scores, axis=1), keys) * (factor * 0.125)
        queries = jnp.concatenate([query_f * head_mask[h] for h in range(2)], axis=0)
        grad_k = dot_tn(jnp.concatenate(scores, axis=0), queries) * 0.125
        outs = jnp.concatenate([grads_f * head_mask[h] for h in range(2)], axis=0)
        grad_v = dot_tn(jnp.concatenate([probs_ref[0], probs_ref[1]], axis=0), outs)
        return grad_q, grad_k, grad_v

    def near_backward(p, carry):
        off = offsets(0, c, p)
        grad_q, grad_k, grad_v = backward(
            kn[:, 0, p].reshape(T, 128), kn[:, 1, p].reshape(T, 128),
            *(a[p].reshape(128, 128) for a in (gn, d2, f2s, q2, g2)), pn.at[p],
        )
        grad_q = grad_q.reshape(2, 64, 128)
        for s in range(2):
            acc[s, 0, p] = near_spread(grad_q[s], off)
        for k, part in enumerate((grad_k, grad_v)):
            part = part.reshape(4, 64, 128)
            for s in range(2):
                acc[s, 1 + k, p] = near_spread(part[s], off)
            for r in range(2):
                nsend[r, k, p] = part[2 + r].astype(BF16)
        return carry

    for p in range(2):
        near_backward(p, 0)
    near_back = []
    for r in range(2):
        copy = remote(nsend.at[r], nrecv.at[r], near_s.at[1, r], near_r.at[1, r], near_pos(r))
        near_back.append(copy)

    def far_backward(p, carry):
        off = offsets(1, c, p)
        grad_q, grad_k, grad_v = backward(
            kf[:, 0, p].reshape(T, 128), kf[:, 1, p].reshape(T, 128),
            *(a[p].reshape(32, 128) for a in (gf, d3, f3s, q3, g3)), pf.at[p],
        )
        grad_q = grad_q.reshape(2, 16, 128)
        for s in range(2):
            acc[s, 0, p] += far_spread(grad_q[s], off)
        for k, part in enumerate((grad_k, grad_v)):
            part = part.reshape(16, 16, 128)
            fown[:, k, p] = part[:8]
            fsend[:, k, p] = part[8:].astype(BF16)
        return carry

    for p in range(2):
        far_backward(p, 0)
    plane_back = remote(fsend, frecv, far_s.at[1, 0], far_r.at[1, 0], at(zp, xx, c))
    plane_back.start()

    def dense_backward(s):
        def body(p, carry):
            grad_parts = backward(
                x[s, 1, p], x[s, 2, p], g[s, p], d1[s, p], f1s[s, p], q1[s, p], g1[s, p],
                p1.at[s, p],
            )
            for t, part in enumerate(grad_parts):
                acc[s, t, p] += part
            return carry

        for p in range(2):
            body(p, 0)

    dense_backward(1)
    plane_back.wait()
    for k in range(2):
        for p in range(2):
            off = offsets(1, c, p)
            both = fown[:, k, p] + frecv[:, k, p].astype(F32)
            for s in range(2):
                acc[s, 1 + k, p] += far_spread(both[s], off)
            fback[:, k, p] = both[2:].astype(BF16)
    sibs[...] = acc[1].astype(BF16)
    sib_back = remote(sibs, sibr, sib_s.at[2], sib_r.at[2], sib)
    sib_back.start()
    far_back = []
    for dx in (2, 1, 3):
        for r in range(2):
            slot = 2 * (dx - 1) + r
            copy = remote(
                fback.at[slot], fhome.at[slot], far_s.at[1, 8 + slot], far_r.at[1, 8 + slot],
                far_pos(0, -dx, r),
            )
            far_back.append(copy)

    dense_backward(0)

    for _, copy in xy_copies:
        copy.wait_send()
    for copy in near_back + far_back:
        copy.start()
    total = wgs[0, xx].astype(F32)
    for slot, copy in reversed(xy_copies):
        copy.wait_recv()
        total = total + wgr[slot].astype(F32)
    for a in range(4):
        for half in range(2):
            chunk = total[a, 8 * half : 8 * half + 8]
            zsb[a, half] = jnp.concatenate([chunk[:, :128], chunk[:, 128:]], axis=0).astype(BF16)
    zy_copies = []
    for dy in (2, 1, 3, 0):
        for a in range(4):
            for half in range(2):
                target = at(4 * c + a, xx, half)
                source, landing = zsb.at[a, half], zr.at[dy, z]
                copy = remote(
                    source, landing, zy_s.at[dy, a, half], zy_r.at[dy, z], target, (y + dy) % YS
                )
                if dy > 0:
                    copy.start()
                else:

                    @pl.when(target != pos)
                    def _(copy=copy):
                        copy.start()

                    @pl.when(target == pos)
                    def _(source=source, landing=landing):
                        pltpu.make_async_copy(source, landing, zy_r.at[0, z]).start()

                zy_copies.append((copy, dy, target))

    for copy in near_back:
        copy.wait()
    for copy in far_back:
        copy.wait()

    def returned(t, p, r):
        half = c if r == 0 else 1 - c
        near = near_spread(nrecv[r, t - 1, p].astype(F32), offsets(0, half, p))
        far = fhome[r, t - 1, p].astype(F32)
        for d in range(1, 3):
            far = far + fhome[2 * d + r, t - 1, p].astype(F32)
        return near + far_spread(far, offsets(1, half, p))

    def write(t, columns, parts):
        joined = jnp.concatenate([part.astype(BF16) for part in parts], axis=1)
        out_ref[t, :, pl.ds(columns, 256)] = dot(perm[...], joined).astype(BF16)

    for t in range(3):
        parts = [acc[0, t, p] for p in range(2)]
        if t > 0:
            parts = [parts[p] + returned(t, p, 0) for p in range(2)]
        write(t, mine, parts)
    sib_back.wait()
    for t in range(3):
        parts = [sibr[t, p].astype(F32) for p in range(2)]
        if t > 0:
            parts = [parts[p] + returned(t, p, 1) for p in range(2)]
        write(t, theirs, parts)
    for copy, dy, target in zy_copies:
        if dy > 0:
            copy.wait_send()
        else:

            @pl.when(target != pos)
            def _(copy=copy):
                copy.wait_send()

    for dy in range(YS):
        total = jnp.zeros((16, 128), F32)
        for k in range(ZS):
            arrived = zr.at[dy, k]
            remote(arrived, arrived, zy_s.at[0, 0, 0], zy_r.at[dy, k], sib).wait_recv()
            total = total + zr[dy, k].astype(F32)
        total = total * (1.0 / YS)
        first = 256 * ((y - dy + YS) % YS)
        wg_ref[:, pl.ds(pl.multiple_of(first, 128), 128)] = total[:8]
        wg_ref[:, pl.ds(pl.multiple_of(first + 128, 128), 128)] = total[8:]


def deliver(grads_ref, weight_ref, out_ref, wg_ref, sem):
    first = pltpu.make_async_copy(grads_ref, out_ref, sem.at[0])
    second = pltpu.make_async_copy(weight_ref, wg_ref, sem.at[1])
    first.start()
    second.start()
    first.wait()
    second.wait()


def local(qkv, dout, out_weight, head_offsets):
    planes = jnp.transpose(qkv[0], (1, 0, 2))
    vmem = pltpu.VMEM
    dma = pltpu.SemaphoreType.DMA
    grads, weight_grad = pl.pallas_call(
        kernel,
        out_shape=(
            pltpu.VMEM((3, T, 512), BF16),
            pltpu.VMEM((8, 1024), F32),
        ),
        in_specs=[
            pl.BlockSpec(memory_space=pltpu.HBM),
            pl.BlockSpec(memory_space=pltpu.HBM),
            pl.BlockSpec(memory_space=pltpu.HBM),
            pl.BlockSpec(memory_space=pltpu.HBM),
        ],
        out_specs=(pl.BlockSpec(memory_space=pltpu.VMEM), pl.BlockSpec(memory_space=pltpu.VMEM)),
        scratch_shapes=[
            vmem((3, T, 512), BF16),
            *[vmem((2, T, 1024), BF16)] * 2,
            vmem((256, 1024), BF16),
            vmem((T, T), BF16),
            vmem((2, 3, 2, T, 128), BF16),
            vmem((3, 2, T, 128), BF16),
            vmem((3, 2, T, 128), BF16),
            vmem((3, 2, T, 128), BF16),
            vmem((4, 2, 2, 64, 128), BF16),
            vmem((2, 2, 64, 128), BF16),
            vmem((16, 2, 2, 16, 128), BF16),
            vmem((2, 2, 16, 128), BF16),
            vmem((2, 2, 64, 128), BF16),
            vmem((2, 2, 16, 128), BF16),
            vmem((2, 2, T, 128), BF16),
            *[vmem((2, 2, T, 128), F32)] * 3,
            *[vmem((2, 2, 64, 128), F32)] * 3,
            *[vmem((2, 2, 16, 128), F32)] * 3,
            vmem((2, 2, 2, T, T), BF16),
            vmem((2, 2, 128, T), BF16),
            vmem((2, 2, 32, T), BF16),
            vmem((256, 2 * T), BF16),
            *[vmem((2, 2, T, 128), BF16)] * 2,
            *[vmem((2, 2, T, 128), F32)] * 2,
            *[vmem((2, 2, 64, 128), BF16)] * 3,
            *[vmem((2, 2, 64, 128), F32)] * 2,
            *[vmem((2, 2, 16, 128), BF16)] * 3,
            *[vmem((2, 2, 16, 128), F32)] * 2,
            vmem((2, 3, 2, T, 128), F32),
            vmem((2, 2, 2, 64, 128), BF16),
            vmem((2, 2, 2, 64, 128), BF16),
            vmem((8, 2, 2, 16, 128), F32),
            *[vmem((8, 2, 2, 16, 128), BF16)] * 2,
            *[vmem((6, 2, 2, 16, 128), BF16)] * 2,
            vmem((4, 4, 4, 16, 256), BF16),
            vmem((15, 4, 16, 256), BF16),
            vmem((4, 2, 16, 128), BF16),
            vmem((4, 8, 16, 128), BF16),
            pltpu.SMEM((2, 8), jnp.int32),
            dma((4,)),
            dma((3,)), dma((3,)),
            dma((2, 2)), dma((2, 2)),
            dma((2, 16)), dma((2, 16)),
            dma((15,)), dma((15,)),
            dma((4, 4, 2)), dma((4, 8)),
            pltpu.SemaphoreType.REGULAR((3,)),
        ],
        compiler_params=pltpu.CompilerParams(
            collective_id=0, has_side_effects=True, vmem_limit_bytes=60 * 1024 * 1024
        ),
        cost_estimate=pl.CostEstimate(
            flops=1_200_000_000, bytes_accessed=4_000_000, transcendentals=700_000
        ),
    )(planes, dout[0], out_weight, head_offsets)
    grads, weight_grad = pl.pallas_call(
        deliver,
        out_shape=(
            jax.ShapeDtypeStruct((3, T, 512), BF16),
            jax.ShapeDtypeStruct((8, 1024), F32),
        ),
        in_specs=[pl.BlockSpec(memory_space=pl.ANY)] * 2,
        out_specs=[pl.BlockSpec(memory_space=pltpu.HBM)] * 2,
        scratch_shapes=[dma((2,))],
        compiler_params=pltpu.CompilerParams(vmem_limit_bytes=2 * 1024 * 1024),
    )(grads, weight_grad)
    return jnp.transpose(grads, (1, 0, 2))[None], weight_grad


def solution(mesh):
    return jax.shard_map(
        local,
        mesh=mesh,
        in_specs=(P("dp", "seq", None, None), P("dp", "seq", None), P(), P()),
        out_specs=(P("dp", "seq", None, None), P("seq", None)),
        check_vma=False,
    )
```

```python
import jax
import jax.numpy as jnp
from jax import lax
from jax.experimental import pallas as pl
from jax.experimental.pallas import tpu as pltpu
from jax.sharding import PartitionSpec as P

XS, ZS, YS = 4, 8, 4
T = 256
E = 64
C2 = 0.125 * 1.4426950408889634
F32, BF16 = jnp.float32, jnp.bfloat16
NEG = -3.0e38


def dot(a, b):
    return lax.dot_general(a, b, (((1,), (0,)), ((), ())), preferred_element_type=F32)


def dot_nt(a, b):
    return lax.dot_general(a, b, (((1,), (1,)), ((), ())), preferred_element_type=F32)


def dot_tn(a, b):
    return lax.dot_general(a, b, (((0,), (0,)), ((), ())), preferred_element_type=F32)


def kernel(
    qkv_ref, dout_ref, w_ref, off_hbm, out_ref, wg_ref,
    qkv_in, dout2, pdout, wv, perm, x, oth, sibs, sibr, kn, ns, kf, fs, qn, qf, g,
    o1, t1, m1, o2, t2, m2, o3, t3, m3, p1, pn, pf, attn,
    lows, f2w, f3w, g1, q1, f1s, d1, gn, g2, q2, f2s, d2, gf, g3, q3, f3s, d3,
    acc, nsend, nrecv, fown, fsend, frecv, fback, fhome, wgs, wgr, zsb, zr, off_ref,
    load_sem, sib_s, sib_r, near_s, near_r, far_s, far_r, xy_s, xy_r, zy_s, zy_r, known,
):
    pos = lax.axis_index("seq")
    y = lax.axis_index("dp")
    c = pos % 2
    xx = (pos // 2) % XS
    z = pos // (2 * XS)

    def at(z_, x_, c_):
        return (z_ * XS + x_) * 2 + c_

    zp = z + 1 - 2 * (z % 2)

    def far_pos(dz, dx, r):
        return at(z if dz == 0 else zp, (xx + dx + XS) % XS, (c + r) % 2)

    def far_peers():
        peers = [(dz, dx, r) for dz in (1, 0) for dx in (2, 1, 3, 0) for r in (0, 1)]
        return [peer for peer in peers if peer[:2] != (0, 0)]

    xp = xx + 1 - 2 * (xx % 2)
    sib = at(z, xx, 1 - c)

    def near_pos(r):
        return at(z, xp, (c + r) % 2)

    z_outer = (z + 2 * (z % 2) - 1 + ZS) % ZS

    def z_pos(d):
        return at((z + d + ZS) % ZS, xx, c)

    def remote(src, dst, send, recv, target, row=None):
        where = {"seq": target} if row is None else {"seq": target, "dp": row}
        return pltpu.make_async_remote_copy(
            src_ref=src, dst_ref=dst, send_sem=send, recv_sem=recv,
            device_id=where, device_id_type=pl.DeviceIdType.MESH,
        )

    mine = pl.multiple_of(c * 256, 256)
    theirs = pl.multiple_of((1 - c) * 256, 256)
    load_qkv = pltpu.make_async_copy(qkv_ref, qkv_in, load_sem.at[0])
    load_dout = pltpu.make_async_copy(dout_ref, dout2.at[0], load_sem.at[1])
    load_w = pltpu.make_async_copy(w_ref.at[pl.ds(mine, 256), :], wv, load_sem.at[2])
    load_off = pltpu.make_async_copy(off_hbm, off_ref, load_sem.at[3])
    load_qkv.start()
    load_off.start()
    load_dout.start()
    load_w.start()

    barrier = pltpu.get_barrier_semaphore()

    def tell(semaphore, target, row=None):
        where = {"seq": target} if row is None else {"seq": target, "dp": row}
        pl.semaphore_signal(
            semaphore, inc=1, device_id=where, device_id_type=pl.DeviceIdType.MESH
        )

    tell(barrier, at(z_outer, xx, c))
    for d in range(1, YS):
        tell(barrier, pos, (y + d) % YS)
    for peer in far_peers():
        tell(barrier, far_pos(*peer))
    tell(barrier, sib)

    lane = lax.broadcasted_iota(jnp.int32, (1, 128), 1)
    low_lane = lane < E
    head_mask = [low_lane.astype(F32).astype(BF16), (lane >= E).astype(F32).astype(BF16)]

    def offsets(row, half, pair):
        first = 4 * half + 2 * pair
        return jnp.where(low_lane, off_ref[row, first], off_ref[row, first + 1])

    def near_rows(array, off):
        shaped = array.reshape(4, 4, 16, 128)
        parts = [shaped[:, k] * (off == k).astype(F32).astype(array.dtype) for k in range(4)]
        return ((parts[0] + parts[1]) + (parts[2] + parts[3])).reshape(64, 128)

    def far_rows(array, off):
        shaped = array.reshape(16, 16, 128)
        total = shaped[0] * (off == 0).astype(F32).astype(array.dtype)
        for k in range(1, 16):
            total = total + shaped[k] * (off == k).astype(F32).astype(array.dtype)
        return total

    def near_spread(array, off):
        shaped = array.reshape(4, 1, 16, 128)
        parts = [jnp.where((off == k).reshape(1, 1, 1, 128), shaped, 0.0) for k in range(4)]
        return jnp.concatenate(parts, axis=1).reshape(T, 128)

    def far_spread(array, off):
        parts = [jnp.where(off == k, array, 0.0) for k in range(16)]
        return jnp.concatenate(parts, axis=0)

    row_id = lax.broadcasted_iota(jnp.int32, (T, T), 0)
    col_id = lax.broadcasted_iota(jnp.int32, (T, T), 1)
    swapped = (row_id % 16) * 16 + row_id // 16
    perm[...] = (swapped == col_id).astype(F32).astype(BF16)

    load_off.wait()
    load_qkv.wait()
    for t in range(3):
        own = dot(perm[...], qkv_in[t, :, pl.ds(mine, 256)]).astype(BF16)
        x[0, t, 0] = own[:, :128]
        x[0, t, 1] = own[:, 128:]
        other = dot(perm[...], qkv_in[t, :, pl.ds(theirs, 256)]).astype(BF16)
        oth[t, 0] = other[:, :128]
        oth[t, 1] = other[:, 128:]
    for p in range(2):
        near_own, far_own = offsets(0, c, p), offsets(1, c, p)
        near_other, far_other = offsets(0, 1 - c, p), offsets(1, 1 - c, p)
        for k in range(2):
            kn[0, k, p] = near_rows(x[0, 1 + k, p], near_own)
            kf[0, k, p] = far_rows(x[0, 1 + k, p], far_own)
            ns[k, p] = near_rows(oth[1 + k, p], near_other)
            fs[k, p] = far_rows(oth[1 + k, p], far_other)
        qn[p, 0] = near_rows(x[0, 0, p], near_own)
        qf[p, 0] = far_rows(x[0, 0, p], far_own)
    pl.semaphore_wait(barrier, 15 + (YS - 1) + 1)

    far_copies = []
    for dz, dx, r in far_peers():
        slot = 8 * dz + 2 * dx + r
        copy = remote(
            kf.at[0] if r == 0 else fs, kf.at[slot],
            far_s.at[0, slot], far_r.at[0, slot], far_pos(dz, dx, r),
        )
        copy.start()
        far_copies.append(copy)
    near_copies = []
    for r in range(2):
        copy = remote(
            kn.at[0] if r == 0 else ns, kn.at[2 + r], near_s.at[0, r], near_r.at[0, r], near_pos(r)
        )
        copy.start()
        near_copies.append(copy)
    sib_copy = remote(oth, x.at[1], sib_s.at[0], sib_r.at[0], sib)
    sib_copy.start()
    load_dout.wait()
    dout_copy = remote(dout2.at[0], dout2.at[1], sib_s.at[1], sib_r.at[1], sib)
    dout_copy.start()
    for d in (-1, 1):
        tell(known.at[0], z_pos(d))

    def forward(query, key, value, probs_ref):
        probs, maxima = [], []
        for h in range(2):
            scores = dot_nt(query, key * head_mask[h])
            row_max = jnp.max(scores, axis=1, keepdims=True)
            prob = jnp.exp2((scores - row_max) * C2).astype(BF16)
            probs_ref[h] = prob
            probs.append(prob)
            maxima.append(row_max * C2)
        ones = jnp.ones((T, 128), BF16)
        right = jnp.concatenate(
            [
                jnp.concatenate([value * head_mask[h], ones * head_mask[h]], axis=1)
                for h in range(2)
            ],
            axis=0,
        )
        both = dot(jnp.concatenate(probs, axis=1), right)
        return both[:, :128], both[:, 128:], jnp.where(low_lane, maxima[0], maxima[1])

    def dense_forward(s):
        def body(p, carry):
            out, total, peak = forward(x[s, 0, p], x[s, 1, p], x[s, 2, p], p1.at[s, p])
            o1[s, p], t1[s, p], m1[s, p] = out, total, peak
            return carry

        for p in range(2):
            body(p, 0)

    def grad_in(s):
        for k in range(4):
            columns = slice(256 * k, 256 * k + 256)
            pdout[s, :, columns] = dot(perm[...], dout2[s, :, columns]).astype(BF16)

    def grad_attn(s):
        moved = dot_nt(pdout[s], wv[...]).astype(BF16)
        g[s, 0] = moved[:, :128]
        g[s, 1] = moved[:, 128:]

    dense_forward(0)
    grad_in(0)
    sib_copy.wait()
    for p in range(2):
        near_own, far_own = offsets(0, c, p), offsets(1, c, p)
        for k in range(2):
            kn[1, k, p] = near_rows(x[1, 1 + k, p], near_own)
            kf[1, k, p] = far_rows(x[1, 1 + k, p], far_own)
        qn[p, 1] = near_rows(x[1, 0, p], near_own)
        qf[p, 1] = far_rows(x[1, 0, p], far_own)
    dense_forward(1)
    pl.semaphore_wait(known.at[0], 2)
    for d in (-2, 2):
        tell(known.at[1], z_pos(d))
    dout_copy.wait()
    grad_in(1)

    for copy in far_copies:
        copy.wait()
    pl.semaphore_wait(known.at[1], 2)
    tell(known.at[2], sib)

    def far_forward(p, carry):
        out, total, peak = forward(
            qf[p].reshape(32, 128), kf[:, 0, p].reshape(T, 128), kf[:, 1, p].reshape(T, 128),
            pf.at[p],
        )
        o3[p], t3[p], m3[p] = (a.reshape(2, 16, 128) for a in (out, total, peak))
        return carry

    for p in range(2):
        far_forward(p, 0)
    for copy in near_copies:
        copy.wait()

    def near_forward(p, carry):
        out, total, peak = forward(
            qn[p].reshape(128, 128), kn[:, 0, p].reshape(T, 128), kn[:, 1, p].reshape(T, 128),
            pn.at[p],
        )
        o2[p], t2[p], m2[p] = (a.reshape(2, 64, 128) for a in (out, total, peak))
        return carry

    for p in range(2):
        near_forward(p, 0)

    same_head = (
        (lax.broadcasted_iota(jnp.int32, (256, 128), 0) % 128 < E)
        == (lax.broadcasted_iota(jnp.int32, (256, 128), 1) < E)
    ).astype(F32).astype(BF16)

    def combine(p, s):
        near_off, far_off = offsets(0, c, p), offsets(1, c, p)

        def near_wide(array):
            return jnp.broadcast_to(array.reshape(4, 1, 16, 128), (4, 4, 16, 128)).reshape(T, 128)

        def far_wide(array):
            return jnp.broadcast_to(array.reshape(1, 16, 128), (16, 16, 128)).reshape(T, 128)

        parts = [
            jnp.where((near_off == k).reshape(1, 1, 1, 128), m2[p, s].reshape(4, 1, 16, 128), NEG)
            for k in range(4)
        ]
        max2 = jnp.concatenate(parts, axis=1).reshape(T, 128)
        max3 = jnp.concatenate([jnp.where(far_off == k, m3[p, s], NEG) for k in range(16)], axis=0)
        max1 = m1[s, p]
        peak = jnp.maximum(jnp.maximum(max1, max2), max3)
        e1, e2, e3 = jnp.exp2(max1 - peak), jnp.exp2(max2 - peak), jnp.exp2(max3 - peak)
        denom = e1 * t1[s, p] + e2 * near_wide(t2[p, s]) + e3 * far_wide(t3[p, s])
        inverse = 1.0 / denom
        f1, f2, f3 = e1 * inverse, e2 * inverse, e3 * inverse
        mixed = f1 * o1[s, p] + f2 * near_wide(o2[p, s]) + f3 * far_wide(o3[p, s])
        low = mixed.astype(BF16)
        lows[s, p] = low
        f1s[s, p], f2w[s, p], f3w[s, p] = f1, f2, f3
        return low

    for s in range(2):
        for p in range(2):
            attn[128 * p : 128 * p + 128, s * T : (s + 1) * T] = jnp.transpose(combine(p, s))

    pl.semaphore_wait(known.at[2], 1)
    xy_copies = []
    for dy in (2, 1, 3, 0):
        ty = (y + dy) % YS
        columns = pl.ds(pl.multiple_of(256 * ty, 256), 256)
        both = dot(attn[...], pdout[:, :, columns].reshape(2 * T, 256))
        shaped = both.astype(BF16).reshape(4, XS, 16, 256)
        for to in range(XS):
            wgs[dy, to] = shaped[:, to]
    for dx, dy in ((2, 2), (2, 1), (2, 3), (1, 2), (3, 2), (2, 0), (0, 2), (1, 1), (1, 3), (3, 1),
                   (3, 3), (1, 0), (3, 0), (0, 1), (0, 3)):
        slot = dx * YS + dy - 1
        tx, ty = (xx + dx) % XS, (y + dy) % YS
        copy = remote(wgs.at[dy, tx], wgr.at[slot], xy_s.at[slot], xy_r.at[slot], at(z, tx, c), ty)
        copy.start()
        xy_copies.append((slot, copy))

    def prepare(p, s):
        near_off, far_off = offsets(0, c, p), offsets(1, c, p)
        low, f1, f2, f3 = lows[s, p], f1s[s, p], f2w[s, p], f3w[s, p]
        grads = g[s, p].astype(F32)
        query = x[s, 0, p].astype(F32)
        product = grads * low.astype(F32)
        high = product.astype(BF16)
        rest = (product - high.astype(F32)).astype(BF16)
        dstat = dot(jnp.concatenate([high, rest], axis=1), same_head)
        g1[s, p] = (grads * f1).astype(BF16)
        q1[s, p] = (query * f1).astype(BF16)
        d1[s, p] = dstat
        near_f, near_g = near_rows(f2, near_off), near_rows(g[s, p], near_off)
        gn[p, s] = near_g
        g2[p, s] = (near_g.astype(F32) * near_f).astype(BF16)
        q2[p, s] = (qn[p, s].astype(F32) * near_f).astype(BF16)
        f2s[p, s] = near_f
        d2[p, s] = near_rows(dstat, near_off)
        far_f, far_g = far_rows(f3, far_off), far_rows(g[s, p], far_off)
        gf[p, s] = far_g
        g3[p, s] = (far_g.astype(F32) * far_f).astype(BF16)
        q3[p, s] = (qf[p, s].astype(F32) * far_f).astype(BF16)
        f3s[p, s] = far_f
        d3[p, s] = far_rows(dstat, far_off)

    load_w.wait()
    for s in range(2):
        grad_attn(s)
        for p in range(2):
            prepare(p, s)

    def backward(key, value, grads, dstat, factor, query_f, grads_f, probs_ref):
        scores = []
        for h in range(2):
            grad_probs = dot_nt(grads, value * head_mask[h])
            column = dstat[:, h * E : h * E + 1]
            scores.append((probs_ref[h].astype(F32) * (grad_probs - column)).astype(BF16))
        keys = jnp.concatenate([key * head_mask[h] for h in range(2)], axis=0)
        grad_q = dot(jnp.concatenate(scores, axis=1), keys) * (factor * 0.125)
        queries = jnp.concatenate([query_f * head_mask[h] for h in range(2)], axis=0)
        grad_k = dot_tn(jnp.concatenate(scores, axis=0), queries) * 0.125
        outs = jnp.concatenate([grads_f * head_mask[h] for h in range(2)], axis=0)
        grad_v = dot_tn(jnp.concatenate([probs_ref[0], probs_ref[1]], axis=0), outs)
        return grad_q, grad_k, grad_v

    def near_backward(p, carry):
        off = offsets(0, c, p)
        grad_q, grad_k, grad_v = backward(
            kn[:, 0, p].reshape(T, 128), kn[:, 1, p].reshape(T, 128),
            *(a[p].reshape(128, 128) for a in (gn, d2, f2s, q2, g2)), pn.at[p],
        )
        grad_q = grad_q.reshape(2, 64, 128)
        for s in range(2):
            acc[s, 0, p] = near_spread(grad_q[s], off)
        for k, part in enumerate((grad_k, grad_v)):
            part = part.reshape(4, 64, 128)
            for s in range(2):
                acc[s, 1 + k, p] = near_spread(part[s], off)
            for r in range(2):
                nsend[r, k, p] = part[2 + r].astype(BF16)
        return carry

    for p in range(2):
        near_backward(p, 0)
    near_back = []
    for r in range(2):
        copy = remote(nsend.at[r], nrecv.at[r], near_s.at[1, r], near_r.at[1, r], near_pos(r))
        near_back.append(copy)

    def far_backward(p, carry):
        off = offsets(1, c, p)
        grad_q, grad_k, grad_v = backward(
            kf[:, 0, p].reshape(T, 128), kf[:, 1, p].reshape(T, 128),
            *(a[p].reshape(32, 128) for a in (gf, d3, f3s, q3, g3)), pf.at[p],
        )
        grad_q = grad_q.reshape(2, 16, 128)
        for s in range(2):
            acc[s, 0, p] += far_spread(grad_q[s], off)
        for k, part in enumerate((grad_k, grad_v)):
            part = part.reshape(16, 16, 128)
            fown[:, k, p] = part[:8]
            fsend[:, k, p] = part[8:].astype(BF16)
        return carry

    for p in range(2):
        far_backward(p, 0)
    plane_back = remote(fsend, frecv, far_s.at[1, 0], far_r.at[1, 0], at(zp, xx, c))
    plane_back.start()

    def dense_backward(s):
        def body(p, carry):
            grad_parts = backward(
                x[s, 1, p], x[s, 2, p], g[s, p], d1[s, p], f1s[s, p], q1[s, p], g1[s, p],
                p1.at[s, p],
            )
            for t, part in enumerate(grad_parts):
                acc[s, t, p] += part
            return carry

        for p in range(2):
            body(p, 0)

    dense_backward(1)
    plane_back.wait()
    for k in range(2):
        for p in range(2):
            off = offsets(1, c, p)
            both = fown[:, k, p] + frecv[:, k, p].astype(F32)
            for s in range(2):
                acc[s, 1 + k, p] += far_spread(both[s], off)
            fback[:, k, p] = both[2:].astype(BF16)
    sibs[...] = acc[1].astype(BF16)
    sib_back = remote(sibs, sibr, sib_s.at[2], sib_r.at[2], sib)
    sib_back.start()
    far_back = []
    for dx in (2, 1, 3):
        for r in range(2):
            slot = 2 * (dx - 1) + r
            copy = remote(
                fback.at[slot], fhome.at[slot], far_s.at[1, 8 + slot], far_r.at[1, 8 + slot],
                far_pos(0, -dx, r),
            )
            far_back.append(copy)

    dense_backward(0)

    for _, copy in xy_copies:
        copy.wait_send()
    for copy in near_back + far_back:
        copy.start()
    total = wgs[0, xx].astype(F32)
    for slot, copy in reversed(xy_copies):
        copy.wait_recv()
        total = total + wgr[slot].astype(F32)
    for a in range(4):
        for half in range(2):
            chunk = total[a, 8 * half : 8 * half + 8]
            zsb[a, half] = jnp.concatenate([chunk[:, :128], chunk[:, 128:]], axis=0).astype(BF16)
    zy_copies = []
    for dy in (2, 1, 3, 0):
        for a in range(4):
            for half in range(2):
                target = at(4 * c + a, xx, half)
                source, landing = zsb.at[a, half], zr.at[dy, z]
                copy = remote(
                    source, landing, zy_s.at[dy, a, half], zy_r.at[dy, z], target, (y + dy) % YS
                )
                if dy > 0:
                    copy.start()
                else:

                    @pl.when(target != pos)
                    def _(copy=copy):
                        copy.start()

                    @pl.when(target == pos)
                    def _(source=source, landing=landing):
                        pltpu.make_async_copy(source, landing, zy_r.at[0, z]).start()

                zy_copies.append((copy, dy, target))

    for copy in near_back:
        copy.wait()
    for copy in far_back:
        copy.wait()

    def returned(t, p, r):
        half = c if r == 0 else 1 - c
        near = near_spread(nrecv[r, t - 1, p].astype(F32), offsets(0, half, p))
        far = fhome[r, t - 1, p].astype(F32)
        for d in range(1, 3):
            far = far + fhome[2 * d + r, t - 1, p].astype(F32)
        return near + far_spread(far, offsets(1, half, p))

    def write(t, columns, parts):
        joined = jnp.concatenate([part.astype(BF16) for part in parts], axis=1)
        out_ref[t, :, pl.ds(columns, 256)] = dot(perm[...], joined).astype(BF16)

    for t in range(3):
        parts = [acc[0, t, p] for p in range(2)]
        if t > 0:
            parts = [parts[p] + returned(t, p, 0) for p in range(2)]
        write(t, mine, parts)
    sib_back.wait()
    for t in range(3):
        parts = [sibr[t, p].astype(F32) for p in range(2)]
        if t > 0:
            parts = [parts[p] + returned(t, p, 1) for p in range(2)]
        write(t, theirs, parts)
    for copy, dy, target in zy_copies:
        if dy > 0:
            copy.wait_send()
        else:

            @pl.when(target != pos)
            def _(copy=copy):
                copy.wait_send()

    for dy in range(YS):
        total = jnp.zeros((16, 128), F32)
        for k in range(ZS):
            arrived = zr.at[dy, k]
            remote(arrived, arrived, zy_s.at[0, 0, 0], zy_r.at[dy, k], sib).wait_recv()
            total = total + zr[dy, k].astype(F32)
        total = total * (1.0 / YS)
        first = 256 * ((y - dy + YS) % YS)
        wg_ref[:, pl.ds(pl.multiple_of(first, 128), 128)] = total[:8]
        wg_ref[:, pl.ds(pl.multiple_of(first + 128, 128), 128)] = total[8:]


def deliver(grads_ref, weight_ref, out_ref, wg_ref, sem):
    first = pltpu.make_async_copy(grads_ref, out_ref, sem.at[0])
    second = pltpu.make_async_copy(weight_ref, wg_ref, sem.at[1])
    first.start()
    second.start()
    first.wait()
    second.wait()


def local(qkv, dout, out_weight, head_offsets):
    planes = jnp.transpose(qkv[0], (1, 0, 2))
    vmem = pltpu.VMEM
    dma = pltpu.SemaphoreType.DMA
    grads, weight_grad = pl.pallas_call(
        kernel,
        out_shape=(
            pltpu.VMEM((3, T, 512), BF16),
            pltpu.VMEM((8, 1024), F32),
        ),
        in_specs=[
            pl.BlockSpec(memory_space=pltpu.HBM),
            pl.BlockSpec(memory_space=pltpu.HBM),
            pl.BlockSpec(memory_space=pltpu.HBM),
            pl.BlockSpec(memory_space=pltpu.HBM),
        ],
        out_specs=(pl.BlockSpec(memory_space=pltpu.VMEM), pl.BlockSpec(memory_space=pltpu.VMEM)),
        scratch_shapes=[
            vmem((3, T, 512), BF16),
            *[vmem((2, T, 1024), BF16)] * 2,
            vmem((256, 1024), BF16),
            vmem((T, T), BF16),
            vmem((2, 3, 2, T, 128), BF16),
            vmem((3, 2, T, 128), BF16),
            vmem((3, 2, T, 128), BF16),
            vmem((3, 2, T, 128), BF16),
            vmem((4, 2, 2, 64, 128), BF16),
            vmem((2, 2, 64, 128), BF16),
            vmem((16, 2, 2, 16, 128), BF16),
            vmem((2, 2, 16, 128), BF16),
            vmem((2, 2, 64, 128), BF16),
            vmem((2, 2, 16, 128), BF16),
            vmem((2, 2, T, 128), BF16),
            *[vmem((2, 2, T, 128), F32)] * 3,
            *[vmem((2, 2, 64, 128), F32)] * 3,
            *[vmem((2, 2, 16, 128), F32)] * 3,
            vmem((2, 2, 2, T, T), BF16),
            vmem((2, 2, 128, T), BF16),
            vmem((2, 2, 32, T), BF16),
            vmem((256, 2 * T), BF16),
            vmem((2, 2, T, 128), BF16),
            *[vmem((2, 2, T, 128), F32)] * 2,
            *[vmem((2, 2, T, 128), BF16)] * 2,
            *[vmem((2, 2, T, 128), F32)] * 2,
            *[vmem((2, 2, 64, 128), BF16)] * 3,
            *[vmem((2, 2, 64, 128), F32)] * 2,
            *[vmem((2, 2, 16, 128), BF16)] * 3,
            *[vmem((2, 2, 16, 128), F32)] * 2,
            vmem((2, 3, 2, T, 128), F32),
            vmem((2, 2, 2, 64, 128), BF16),
            vmem((2, 2, 2, 64, 128), BF16),
            vmem((8, 2, 2, 16, 128), F32),
            *[vmem((8, 2, 2, 16, 128), BF16)] * 2,
            *[vmem((6, 2, 2, 16, 128), BF16)] * 2,
            vmem((4, 4, 4, 16, 256), BF16),
            vmem((15, 4, 16, 256), BF16),
            vmem((4, 2, 16, 128), BF16),
            vmem((4, 8, 16, 128), BF16),
            pltpu.SMEM((2, 8), jnp.int32),
            dma((4,)),
            dma((3,)), dma((3,)),
            dma((2, 2)), dma((2, 2)),
            dma((2, 16)), dma((2, 16)),
            dma((15,)), dma((15,)),
            dma((4, 4, 2)), dma((4, 8)),
            pltpu.SemaphoreType.REGULAR((3,)),
        ],
        compiler_params=pltpu.CompilerParams(
            collective_id=0, has_side_effects=True, vmem_limit_bytes=60 * 1024 * 1024
        ),
        cost_estimate=pl.CostEstimate(
            flops=1_200_000_000, bytes_accessed=4_000_000, transcendentals=700_000
        ),
    )(planes, dout[0], out_weight, head_offsets)
    grads, weight_grad = pl.pallas_call(
        deliver,
        out_shape=(
            jax.ShapeDtypeStruct((3, T, 512), BF16),
            jax.ShapeDtypeStruct((8, 1024), F32),
        ),
        in_specs=[pl.BlockSpec(memory_space=pl.ANY)] * 2,
        out_specs=[pl.BlockSpec(memory_space=pltpu.HBM)] * 2,
        scratch_shapes=[dma((2,))],
        compiler_params=pltpu.CompilerParams(vmem_limit_bytes=2 * 1024 * 1024),
    )(grads, weight_grad)
    return jnp.transpose(grads, (1, 0, 2))[None], weight_grad


def solution(mesh):
    return jax.shard_map(
        local,
        mesh=mesh,
        in_specs=(P("dp", "seq", None, None), P("dp", "seq", None), P(), P()),
        out_specs=(P("dp", "seq", None, None), P("seq", None)),
        check_vma=False,
    )
```

```python
import jax
import jax.numpy as jnp
from jax import lax
from jax.experimental import pallas as pl
from jax.experimental.pallas import tpu as pltpu
from jax.sharding import PartitionSpec as P

XS, ZS, YS = 4, 8, 4
T = 256
E = 64
C2 = 0.125 * 1.4426950408889634
F32, BF16 = jnp.float32, jnp.bfloat16
NEG = -3.0e38


def dot(a, b):
    return lax.dot_general(a, b, (((1,), (0,)), ((), ())), preferred_element_type=F32)


def dot_nt(a, b):
    return lax.dot_general(a, b, (((1,), (1,)), ((), ())), preferred_element_type=F32)


def dot_tn(a, b):
    return lax.dot_general(a, b, (((0,), (0,)), ((), ())), preferred_element_type=F32)


def kernel(
    qkv_ref, dout_ref, w_ref, off_hbm, out_ref, wg_ref,
    qkv_in, dout2, pdout, wv, perm, x, oth, sibs, sibr, kn, ns, kf, fs, qn, qf, g,
    o1, t1, m1, o2, t2, m2, o3, t3, m3, p1, pn, pf, attn,
    lows, f2w, f3w, g1, q1, f1s, d1, gn, g2, q2, f2s, d2, gf, g3, q3, f3s, d3,
    acc, nsend, nrecv, fown, fsend, frecv, fback, fhome, wgs, wgr, zsb, zr, off_ref,
    load_sem, sib_s, sib_r, near_s, near_r, far_s, far_r, xy_s, xy_r, zy_s, zy_r, known,
):
    pos = lax.axis_index("seq")
    y = lax.axis_index("dp")
    c = pos % 2
    xx = (pos // 2) % XS
    z = pos // (2 * XS)

    def at(z_, x_, c_):
        return (z_ * XS + x_) * 2 + c_

    zp = z + 1 - 2 * (z % 2)

    def far_pos(dz, dx, r):
        return at(z if dz == 0 else zp, (xx + dx + XS) % XS, (c + r) % 2)

    def far_peers():
        peers = [(dz, dx, r) for dz in (1, 0) for dx in (2, 1, 3, 0) for r in (0, 1)]
        return [peer for peer in peers if peer[:2] != (0, 0)]

    xp = xx + 1 - 2 * (xx % 2)
    sib = at(z, xx, 1 - c)

    def near_pos(r):
        return at(z, xp, (c + r) % 2)

    z_outer = (z + 2 * (z % 2) - 1 + ZS) % ZS

    def z_pos(d):
        return at((z + d + ZS) % ZS, xx, c)

    def remote(src, dst, send, recv, target, row=None):
        where = {"seq": target} if row is None else {"seq": target, "dp": row}
        return pltpu.make_async_remote_copy(
            src_ref=src, dst_ref=dst, send_sem=send, recv_sem=recv,
            device_id=where, device_id_type=pl.DeviceIdType.MESH,
        )

    mine = pl.multiple_of(c * 256, 256)
    theirs = pl.multiple_of((1 - c) * 256, 256)
    load_qkv = pltpu.make_async_copy(qkv_ref, qkv_in, load_sem.at[0])
    load_dout = pltpu.make_async_copy(dout_ref, dout2.at[0], load_sem.at[1])
    load_w = pltpu.make_async_copy(w_ref.at[pl.ds(mine, 256), :], wv, load_sem.at[2])
    load_off = pltpu.make_async_copy(off_hbm, off_ref, load_sem.at[3])
    load_qkv.start()
    load_off.start()
    load_dout.start()
    load_w.start()

    barrier = pltpu.get_barrier_semaphore()

    def tell(semaphore, target, row=None):
        where = {"seq": target} if row is None else {"seq": target, "dp": row}
        pl.semaphore_signal(
            semaphore, inc=1, device_id=where, device_id_type=pl.DeviceIdType.MESH
        )

    tell(barrier, at(z_outer, xx, c))
    for d in range(1, YS):
        tell(barrier, pos, (y + d) % YS)
    for peer in far_peers():
        tell(barrier, far_pos(*peer))
    tell(barrier, sib)

    lane = lax.broadcasted_iota(jnp.int32, (1, 128), 1)
    low_lane = lane < E
    head_mask = [low_lane.astype(F32).astype(BF16), (lane >= E).astype(F32).astype(BF16)]

    def offsets(row, half, pair):
        first = 4 * half + 2 * pair
        return jnp.where(low_lane, off_ref[row, first], off_ref[row, first + 1])

    def near_rows(array, off):
        shaped = array.reshape(4, 4, 16, 128)
        parts = [shaped[:, k] * (off == k).astype(F32).astype(array.dtype) for k in range(4)]
        return ((parts[0] + parts[1]) + (parts[2] + parts[3])).reshape(64, 128)

    def far_rows(array, off):
        shaped = array.reshape(16, 16, 128)
        total = shaped[0] * (off == 0).astype(F32).astype(array.dtype)
        for k in range(1, 16):
            total = total + shaped[k] * (off == k).astype(F32).astype(array.dtype)
        return total

    def near_spread(array, off):
        shaped = array.reshape(4, 1, 16, 128)
        parts = [jnp.where((off == k).reshape(1, 1, 1, 128), shaped, 0.0) for k in range(4)]
        return jnp.concatenate(parts, axis=1).reshape(T, 128)

    def far_spread(array, off):
        parts = [jnp.where(off == k, array, 0.0) for k in range(16)]
        return jnp.concatenate(parts, axis=0)

    row_id = lax.broadcasted_iota(jnp.int32, (T, T), 0)
    col_id = lax.broadcasted_iota(jnp.int32, (T, T), 1)
    swapped = (row_id % 16) * 16 + row_id // 16
    perm[...] = (swapped == col_id).astype(F32).astype(BF16)

    load_off.wait()
    load_qkv.wait()
    for t in range(3):
        own = dot(perm[...], qkv_in[t, :, pl.ds(mine, 256)]).astype(BF16)
        x[0, t, 0] = own[:, :128]
        x[0, t, 1] = own[:, 128:]
        other = dot(perm[...], qkv_in[t, :, pl.ds(theirs, 256)]).astype(BF16)
        oth[t, 0] = other[:, :128]
        oth[t, 1] = other[:, 128:]
    for p in range(2):
        near_own, far_own = offsets(0, c, p), offsets(1, c, p)
        near_other, far_other = offsets(0, 1 - c, p), offsets(1, 1 - c, p)
        for k in range(2):
            kn[0, k, p] = near_rows(x[0, 1 + k, p], near_own)
            kf[0, k, p] = far_rows(x[0, 1 + k, p], far_own)
            ns[k, p] = near_rows(oth[1 + k, p], near_other)
            fs[k, p] = far_rows(oth[1 + k, p], far_other)
        qn[p, 0] = near_rows(x[0, 0, p], near_own)
        qf[p, 0] = far_rows(x[0, 0, p], far_own)
    pl.semaphore_wait(barrier, 15 + (YS - 1) + 1)

    far_copies = []
    for dz, dx, r in far_peers():
        slot = 8 * dz + 2 * dx + r
        copy = remote(
            kf.at[0] if r == 0 else fs, kf.at[slot],
            far_s.at[0, slot], far_r.at[0, slot], far_pos(dz, dx, r),
        )
        copy.start()
        far_copies.append(copy)
    near_copies = []
    for r in range(2):
        copy = remote(
            kn.at[0] if r == 0 else ns, kn.at[2 + r], near_s.at[0, r], near_r.at[0, r], near_pos(r)
        )
        copy.start()
        near_copies.append(copy)
    sib_copy = remote(oth, x.at[1], sib_s.at[0], sib_r.at[0], sib)
    sib_copy.start()
    load_dout.wait()
    dout_copy = remote(dout2.at[0], dout2.at[1], sib_s.at[1], sib_r.at[1], sib)
    dout_copy.start()
    for d in (-1, 1):
        tell(known.at[0], z_pos(d))

    def forward(query, key, value, probs_ref):
        probs, maxima = [], []
        for h in range(2):
            scores = dot_nt(query, key * head_mask[h])
            row_max = jnp.max(scores, axis=1, keepdims=True)
            prob = jnp.exp2((scores - row_max) * C2).astype(BF16)
            probs_ref[h] = prob
            probs.append(prob)
            maxima.append(row_max * C2)
        ones = jnp.ones((T, 128), BF16)
        right = jnp.concatenate(
            [
                jnp.concatenate([value * head_mask[h], ones * head_mask[h]], axis=1)
                for h in range(2)
            ],
            axis=0,
        )
        both = dot(jnp.concatenate(probs, axis=1), right)
        return both[:, :128], both[:, 128:], jnp.where(low_lane, maxima[0], maxima[1])

    def dense_forward(s):
        def body(p, carry):
            out, total, peak = forward(x[s, 0, p], x[s, 1, p], x[s, 2, p], p1.at[s, p])
            o1[s, p], t1[s, p], m1[s, p] = out, total, peak
            return carry

        for p in range(2):
            body(p, 0)

    def grad_in(s):
        for k in range(4):
            columns = slice(256 * k, 256 * k + 256)
            pdout[s, :, columns] = dot(perm[...], dout2[s, :, columns]).astype(BF16)

    def grad_attn(s):
        moved = dot_nt(pdout[s], wv[...]).astype(BF16)
        g[s, 0] = moved[:, :128]
        g[s, 1] = moved[:, 128:]

    dense_forward(0)
    sib_copy.wait()
    for p in range(2):
        near_own, far_own = offsets(0, c, p), offsets(1, c, p)
        for k in range(2):
            kn[1, k, p] = near_rows(x[1, 1 + k, p], near_own)
            kf[1, k, p] = far_rows(x[1, 1 + k, p], far_own)
        qn[p, 1] = near_rows(x[1, 0, p], near_own)
        qf[p, 1] = far_rows(x[1, 0, p], far_own)
    dense_forward(1)
    pl.semaphore_wait(known.at[0], 2)
    for d in (-2, 2):
        tell(known.at[1], z_pos(d))

    for copy in far_copies:
        copy.wait()
    pl.semaphore_wait(known.at[1], 2)
    tell(known.at[2], sib)

    def far_forward(p, carry):
        out, total, peak = forward(
            qf[p].reshape(32, 128), kf[:, 0, p].reshape(T, 128), kf[:, 1, p].reshape(T, 128),
            pf.at[p],
        )
        o3[p], t3[p], m3[p] = (a.reshape(2, 16, 128) for a in (out, total, peak))
        return carry

    for p in range(2):
        far_forward(p, 0)
    grad_in(0)
    dout_copy.wait()
    grad_in(1)
    for copy in near_copies:
        copy.wait()

    def near_forward(p, carry):
        out, total, peak = forward(
            qn[p].reshape(128, 128), kn[:, 0, p].reshape(T, 128), kn[:, 1, p].reshape(T, 128),
            pn.at[p],
        )
        o2[p], t2[p], m2[p] = (a.reshape(2, 64, 128) for a in (out, total, peak))
        return carry

    for p in range(2):
        near_forward(p, 0)

    same_head = (
        (lax.broadcasted_iota(jnp.int32, (256, 128), 0) % 128 < E)
        == (lax.broadcasted_iota(jnp.int32, (256, 128), 1) < E)
    ).astype(F32).astype(BF16)

    def combine(p, s):
        near_off, far_off = offsets(0, c, p), offsets(1, c, p)

        def near_wide(array):
            return jnp.broadcast_to(array.reshape(4, 1, 16, 128), (4, 4, 16, 128)).reshape(T, 128)

        def far_wide(array):
            return jnp.broadcast_to(array.reshape(1, 16, 128), (16, 16, 128)).reshape(T, 128)

        parts = [
            jnp.where((near_off == k).reshape(1, 1, 1, 128), m2[p, s].reshape(4, 1, 16, 128), NEG)
            for k in range(4)
        ]
        max2 = jnp.concatenate(parts, axis=1).reshape(T, 128)
        max3 = jnp.concatenate([jnp.where(far_off == k, m3[p, s], NEG) for k in range(16)], axis=0)
        max1 = m1[s, p]
        peak = jnp.maximum(jnp.maximum(max1, max2), max3)
        e1, e2, e3 = jnp.exp2(max1 - peak), jnp.exp2(max2 - peak), jnp.exp2(max3 - peak)
        denom = e1 * t1[s, p] + e2 * near_wide(t2[p, s]) + e3 * far_wide(t3[p, s])
        inverse = 1.0 / denom
        f1, f2, f3 = e1 * inverse, e2 * inverse, e3 * inverse
        mixed = f1 * o1[s, p] + f2 * near_wide(o2[p, s]) + f3 * far_wide(o3[p, s])
        low = mixed.astype(BF16)
        lows[s, p] = low
        f1s[s, p], f2w[s, p], f3w[s, p] = f1, f2, f3
        return low

    for s in range(2):
        for p in range(2):
            attn[128 * p : 128 * p + 128, s * T : (s + 1) * T] = jnp.transpose(combine(p, s))

    pl.semaphore_wait(known.at[2], 1)
    xy_copies = []
    for dy in (2, 1, 3, 0):
        ty = (y + dy) % YS
        columns = pl.ds(pl.multiple_of(256 * ty, 256), 256)
        both = dot(attn[...], pdout[:, :, columns].reshape(2 * T, 256))
        shaped = both.astype(BF16).reshape(4, XS, 16, 256)
        for to in range(XS):
            wgs[dy, to] = shaped[:, to]
    for dx, dy in ((2, 2), (2, 1), (2, 3), (1, 2), (3, 2), (2, 0), (0, 2), (1, 1), (1, 3), (3, 1),
                   (3, 3), (1, 0), (3, 0), (0, 1), (0, 3)):
        slot = dx * YS + dy - 1
        tx, ty = (xx + dx) % XS, (y + dy) % YS
        copy = remote(wgs.at[dy, tx], wgr.at[slot], xy_s.at[slot], xy_r.at[slot], at(z, tx, c), ty)
        copy.start()
        xy_copies.append((slot, copy))

    def prepare(p, s):
        near_off, far_off = offsets(0, c, p), offsets(1, c, p)
        low, f1, f2, f3 = lows[s, p], f1s[s, p], f2w[s, p], f3w[s, p]
        grads = g[s, p].astype(F32)
        query = x[s, 0, p].astype(F32)
        product = grads * low.astype(F32)
        high = product.astype(BF16)
        rest = (product - high.astype(F32)).astype(BF16)
        dstat = dot(jnp.concatenate([high, rest], axis=1), same_head)
        g1[s, p] = (grads * f1).astype(BF16)
        q1[s, p] = (query * f1).astype(BF16)
        d1[s, p] = dstat
        near_f, near_g = near_rows(f2, near_off), near_rows(g[s, p], near_off)
        gn[p, s] = near_g
        g2[p, s] = (near_g.astype(F32) * near_f).astype(BF16)
        q2[p, s] = (qn[p, s].astype(F32) * near_f).astype(BF16)
        f2s[p, s] = near_f
        d2[p, s] = near_rows(dstat, near_off)
        far_f, far_g = far_rows(f3, far_off), far_rows(g[s, p], far_off)
        gf[p, s] = far_g
        g3[p, s] = (far_g.astype(F32) * far_f).astype(BF16)
        q3[p, s] = (qf[p, s].astype(F32) * far_f).astype(BF16)
        f3s[p, s] = far_f
        d3[p, s] = far_rows(dstat, far_off)

    load_w.wait()
    for s in range(2):
        grad_attn(s)
        for p in range(2):
            prepare(p, s)

    def backward(key, value, grads, dstat, factor, query_f, grads_f, probs_ref):
        scores = []
        for h in range(2):
            grad_probs = dot_nt(grads, value * head_mask[h])
            column = dstat[:, h * E : h * E + 1]
            scores.append((probs_ref[h].astype(F32) * (grad_probs - column)).astype(BF16))
        keys = jnp.concatenate([key * head_mask[h] for h in range(2)], axis=0)
        grad_q = dot(jnp.concatenate(scores, axis=1), keys) * (factor * 0.125)
        queries = jnp.concatenate([query_f * head_mask[h] for h in range(2)], axis=0)
        grad_k = dot_tn(jnp.concatenate(scores, axis=0), queries) * 0.125
        outs = jnp.concatenate([grads_f * head_mask[h] for h in range(2)], axis=0)
        grad_v = dot_tn(jnp.concatenate([probs_ref[0], probs_ref[1]], axis=0), outs)
        return grad_q, grad_k, grad_v

    def near_backward(p, carry):
        off = offsets(0, c, p)
        grad_q, grad_k, grad_v = backward(
            kn[:, 0, p].reshape(T, 128), kn[:, 1, p].reshape(T, 128),
            *(a[p].reshape(128, 128) for a in (gn, d2, f2s, q2, g2)), pn.at[p],
        )
        grad_q = grad_q.reshape(2, 64, 128)
        for s in range(2):
            acc[s, 0, p] = near_spread(grad_q[s], off)
        for k, part in enumerate((grad_k, grad_v)):
            part = part.reshape(4, 64, 128)
            for s in range(2):
                acc[s, 1 + k, p] = near_spread(part[s], off)
            for r in range(2):
                nsend[r, k, p] = part[2 + r].astype(BF16)
        return carry

    for p in range(2):
        near_backward(p, 0)
    near_back = []
    for r in range(2):
        copy = remote(nsend.at[r], nrecv.at[r], near_s.at[1, r], near_r.at[1, r], near_pos(r))
        near_back.append(copy)

    def far_backward(p, carry):
        off = offsets(1, c, p)
        grad_q, grad_k, grad_v = backward(
            kf[:, 0, p].reshape(T, 128), kf[:, 1, p].reshape(T, 128),
            *(a[p].reshape(32, 128) for a in (gf, d3, f3s, q3, g3)), pf.at[p],
        )
        grad_q = grad_q.reshape(2, 16, 128)
        for s in range(2):
            acc[s, 0, p] += far_spread(grad_q[s], off)
        for k, part in enumerate((grad_k, grad_v)):
            part = part.reshape(16, 16, 128)
            fown[:, k, p] = part[:8]
            fsend[:, k, p] = part[8:].astype(BF16)
        return carry

    for p in range(2):
        far_backward(p, 0)
    plane_back = remote(fsend, frecv, far_s.at[1, 0], far_r.at[1, 0], at(zp, xx, c))
    plane_back.start()

    def dense_backward(s):
        def body(p, carry):
            grad_parts = backward(
                x[s, 1, p], x[s, 2, p], g[s, p], d1[s, p], f1s[s, p], q1[s, p], g1[s, p],
                p1.at[s, p],
            )
            for t, part in enumerate(grad_parts):
                acc[s, t, p] += part
            return carry

        for p in range(2):
            body(p, 0)

    dense_backward(1)
    plane_back.wait()
    for k in range(2):
        for p in range(2):
            off = offsets(1, c, p)
            both = fown[:, k, p] + frecv[:, k, p].astype(F32)
            for s in range(2):
                acc[s, 1 + k, p] += far_spread(both[s], off)
            fback[:, k, p] = both[2:].astype(BF16)
    sibs[...] = acc[1].astype(BF16)
    sib_back = remote(sibs, sibr, sib_s.at[2], sib_r.at[2], sib)
    sib_back.start()
    far_back = []
    for dx in (2, 1, 3):
        for r in range(2):
            slot = 2 * (dx - 1) + r
            copy = remote(
                fback.at[slot], fhome.at[slot], far_s.at[1, 8 + slot], far_r.at[1, 8 + slot],
                far_pos(0, -dx, r),
            )
            far_back.append(copy)

    dense_backward(0)

    for _, copy in xy_copies:
        copy.wait_send()
    for copy in near_back + far_back:
        copy.start()
    total = wgs[0, xx].astype(F32)
    for slot, copy in reversed(xy_copies):
        copy.wait_recv()
        total = total + wgr[slot].astype(F32)
    for a in range(4):
        for half in range(2):
            chunk = total[a, 8 * half : 8 * half + 8]
            zsb[a, half] = jnp.concatenate([chunk[:, :128], chunk[:, 128:]], axis=0).astype(BF16)
    zy_copies = []
    for dy in (2, 1, 3, 0):
        for a in range(4):
            for half in range(2):
                target = at(4 * c + a, xx, half)
                source, landing = zsb.at[a, half], zr.at[dy, z]
                copy = remote(
                    source, landing, zy_s.at[dy, a, half], zy_r.at[dy, z], target, (y + dy) % YS
                )
                if dy > 0:
                    copy.start()
                else:

                    @pl.when(target != pos)
                    def _(copy=copy):
                        copy.start()

                    @pl.when(target == pos)
                    def _(source=source, landing=landing):
                        pltpu.make_async_copy(source, landing, zy_r.at[0, z]).start()

                zy_copies.append((copy, dy, target))

    for copy in near_back:
        copy.wait()
    for copy in far_back:
        copy.wait()

    def returned(t, p, r):
        half = c if r == 0 else 1 - c
        near = near_spread(nrecv[r, t - 1, p].astype(F32), offsets(0, half, p))
        far = fhome[r, t - 1, p].astype(F32)
        for d in range(1, 3):
            far = far + fhome[2 * d + r, t - 1, p].astype(F32)
        return near + far_spread(far, offsets(1, half, p))

    def write(t, columns, parts):
        joined = jnp.concatenate([part.astype(BF16) for part in parts], axis=1)
        out_ref[t, :, pl.ds(columns, 256)] = dot(perm[...], joined).astype(BF16)

    for t in range(3):
        parts = [acc[0, t, p] for p in range(2)]
        if t > 0:
            parts = [parts[p] + returned(t, p, 0) for p in range(2)]
        write(t, mine, parts)
    sib_back.wait()
    for t in range(3):
        parts = [sibr[t, p].astype(F32) for p in range(2)]
        if t > 0:
            parts = [parts[p] + returned(t, p, 1) for p in range(2)]
        write(t, theirs, parts)
    for copy, dy, target in zy_copies:
        if dy > 0:
            copy.wait_send()
        else:

            @pl.when(target != pos)
            def _(copy=copy):
                copy.wait_send()

    for dy in range(YS):
        total = jnp.zeros((16, 128), F32)
        for k in range(ZS):
            arrived = zr.at[dy, k]
            remote(arrived, arrived, zy_s.at[0, 0, 0], zy_r.at[dy, k], sib).wait_recv()
            total = total + zr[dy, k].astype(F32)
        total = total * (1.0 / YS)
        first = 256 * ((y - dy + YS) % YS)
        wg_ref[:, pl.ds(pl.multiple_of(first, 128), 128)] = total[:8]
        wg_ref[:, pl.ds(pl.multiple_of(first + 128, 128), 128)] = total[8:]


def deliver(grads_ref, weight_ref, out_ref, wg_ref, sem):
    first = pltpu.make_async_copy(grads_ref, out_ref, sem.at[0])
    second = pltpu.make_async_copy(weight_ref, wg_ref, sem.at[1])
    first.start()
    second.start()
    first.wait()
    second.wait()


def local(qkv, dout, out_weight, head_offsets):
    planes = jnp.transpose(qkv[0], (1, 0, 2))
    vmem = pltpu.VMEM
    dma = pltpu.SemaphoreType.DMA
    grads, weight_grad = pl.pallas_call(
        kernel,
        out_shape=(
            pltpu.VMEM((3, T, 512), BF16),
            pltpu.VMEM((8, 1024), F32),
        ),
        in_specs=[
            pl.BlockSpec(memory_space=pltpu.HBM),
            pl.BlockSpec(memory_space=pltpu.HBM),
            pl.BlockSpec(memory_space=pltpu.HBM),
            pl.BlockSpec(memory_space=pltpu.HBM),
        ],
        out_specs=(pl.BlockSpec(memory_space=pltpu.VMEM), pl.BlockSpec(memory_space=pltpu.VMEM)),
        scratch_shapes=[
            vmem((3, T, 512), BF16),
            *[vmem((2, T, 1024), BF16)] * 2,
            vmem((256, 1024), BF16),
            vmem((T, T), BF16),
            vmem((2, 3, 2, T, 128), BF16),
            vmem((3, 2, T, 128), BF16),
            vmem((3, 2, T, 128), BF16),
            vmem((3, 2, T, 128), BF16),
            vmem((4, 2, 2, 64, 128), BF16),
            vmem((2, 2, 64, 128), BF16),
            vmem((16, 2, 2, 16, 128), BF16),
            vmem((2, 2, 16, 128), BF16),
            vmem((2, 2, 64, 128), BF16),
            vmem((2, 2, 16, 128), BF16),
            vmem((2, 2, T, 128), BF16),
            *[vmem((2, 2, T, 128), F32)] * 3,
            *[vmem((2, 2, 64, 128), F32)] * 3,
            *[vmem((2, 2, 16, 128), F32)] * 3,
            vmem((2, 2, 2, T, T), BF16),
            vmem((2, 2, 128, T), BF16),
            vmem((2, 2, 32, T), BF16),
            vmem((256, 2 * T), BF16),
            vmem((2, 2, T, 128), BF16),
            *[vmem((2, 2, T, 128), F32)] * 2,
            *[vmem((2, 2, T, 128), BF16)] * 2,
            *[vmem((2, 2, T, 128), F32)] * 2,
            *[vmem((2, 2, 64, 128), BF16)] * 3,
            *[vmem((2, 2, 64, 128), F32)] * 2,
            *[vmem((2, 2, 16, 128), BF16)] * 3,
            *[vmem((2, 2, 16, 128), F32)] * 2,
            vmem((2, 3, 2, T, 128), F32),
            vmem((2, 2, 2, 64, 128), BF16),
            vmem((2, 2, 2, 64, 128), BF16),
            vmem((8, 2, 2, 16, 128), F32),
            *[vmem((8, 2, 2, 16, 128), BF16)] * 2,
            *[vmem((6, 2, 2, 16, 128), BF16)] * 2,
            vmem((4, 4, 4, 16, 256), BF16),
            vmem((15, 4, 16, 256), BF16),
            vmem((4, 2, 16, 128), BF16),
            vmem((4, 8, 16, 128), BF16),
            pltpu.SMEM((2, 8), jnp.int32),
            dma((4,)),
            dma((3,)), dma((3,)),
            dma((2, 2)), dma((2, 2)),
            dma((2, 16)), dma((2, 16)),
            dma((15,)), dma((15,)),
            dma((4, 4, 2)), dma((4, 8)),
            pltpu.SemaphoreType.REGULAR((3,)),
        ],
        compiler_params=pltpu.CompilerParams(
            collective_id=0, has_side_effects=True, vmem_limit_bytes=60 * 1024 * 1024
        ),
        cost_estimate=pl.CostEstimate(
            flops=1_200_000_000, bytes_accessed=4_000_000, transcendentals=700_000
        ),
    )(planes, dout[0], out_weight, head_offsets)
    grads, weight_grad = pl.pallas_call(
        deliver,
        out_shape=(
            jax.ShapeDtypeStruct((3, T, 512), BF16),
            jax.ShapeDtypeStruct((8, 1024), F32),
        ),
        in_specs=[pl.BlockSpec(memory_space=pl.ANY)] * 2,
        out_specs=[pl.BlockSpec(memory_space=pltpu.HBM)] * 2,
        scratch_shapes=[dma((2,))],
        compiler_params=pltpu.CompilerParams(vmem_limit_bytes=2 * 1024 * 1024),
    )(grads, weight_grad)
    return jnp.transpose(grads, (1, 0, 2))[None], weight_grad


def solution(mesh):
    return jax.shard_map(
        local,
        mesh=mesh,
        in_specs=(P("dp", "seq", None, None), P("dp", "seq", None), P(), P()),
        out_specs=(P("dp", "seq", None, None), P("seq", None)),
        check_vma=False,
    )
```
